32 devices in a mesh: dp: 4 (over y, x), seq: 8 (over z, core).
Axes of the slice: x: 2, y: 2, z: 4, core: 2. Of those that a mesh axis runs over, the one named last changes fastest.
Arguments:
- video: bfloat16 [4, 8, 16, 160, 256], P('dp', 'seq'), may hold values from -6 to 6
- cotangent: bfloat16 [4, 8, 16, 160, 256], P('dp', 'seq'), may hold values from -6 to 6
- spatial_weight: bfloat16 [3, 3, 256, 256], replicated, may hold values from -0.125 to 0.125
- temporal_weight: bfloat16 [3, 256, 256], replicated, may hold values from -0.21875 to 0.21875
Outputs:
- video_grad: bfloat16 [4, 8, 16, 160, 256], P('dp', 'seq')
- spatial_grad: float32 [2304, 256], P('seq')
- temporal_grad: float32 [768, 256], P('seq')
The draws below stay inside these ranges and needn't reach their ends.
All inputs are finite; a program needn't handle non-finite values.
Results may differ from the reference program's by a relative error of at most 0.0054.
Values may be sent and summed in bfloat16 or wider, within the bound.
No kernel may reach another device: no remote copies, remote signals or barrier semaphores. Data moves between devices by JAX's collectives and lax.ppermute only.
A program may use at most 128 MiB of HBM per device.

```python
import jax
import jax.numpy as jnp
from jax import lax

C = 256
W = 160
H = 16
FRAMES = 8
CLIPS = 4


def raised(values, key, source, target, shards_of, factor):
    def block_of(position):
        return (jnp.arange(values.shape[position]) // (values.shape[position] // shards_of)).reshape((-1,) + (1,) * (values.ndim - 1 - position))

    first = jax.random.permutation(key, shards_of)[block_of(target)]
    other_side = (block_of(target) + shards_of // 2) % shards_of
    return jnp.where((block_of(source) == first) | (block_of(source) == other_side), factor * values, values)


def shard_levels(rng, dims, split, least, high):
    def one(position, blocks):
        heights = jax.random.uniform(jax.random.fold_in(jax.random.fold_in(rng, 6), position), (blocks,), jnp.float32, least / len(split), high / len(split))
        return jnp.repeat(jnp.exp(heights), dims[position] // blocks).reshape((-1,) + (1,) * (len(dims) - position - 1))

    level = one(*split[0])
    for cut in split[1:]:
        level = level * one(*cut)
    return level


def centred(own_key, extent, width, most, split=(), held_as=jnp.bfloat16):
    loudness = shard_levels(own_key, extent, split, -0.22, 0.18) if split else 1.0
    result = jax.random.normal(own_key, extent, jnp.float32) * width * loudness
    return jnp.minimum(jnp.maximum(result, -most), most).astype(held_as)


def noise_with(rng, dims, deviation, bound, shards, heavy, held_as=jnp.bfloat16):
    array = deviation * jax.random.normal(rng, dims, jnp.float32)
    if shards:
        array = array * shard_levels(rng, dims, shards, -0.22, 0.18)
    return jnp.clip(raised(array, jax.random.fold_in(rng, 3), *heavy), -bound, bound).astype(held_as)


def setup_inputs(seed: int = 0) -> dict:
    keys = jax.random.split(jax.random.key(seed), 5)
    video = noise_with(keys[0], (CLIPS, FRAMES, H, W, C), 1.0, 6.0, ((0, 4), (1, 8)), (1, 4, 8, 2.0))
    cotangent = centred(keys[1], (CLIPS, FRAMES, H, W, C), 1.0, 6.0, ((0, 4), (1, 8)))
    spatial_weight = centred(keys[2], (3, 3, C, C), (9 * C) ** -0.5, 0.125)
    temporal_weight = centred(keys[3], (3, C, C), (3 * C) ** -0.5, 0.21875)
    return {"video": video, "cotangent": cotangent, "spatial_weight": spatial_weight, "temporal_weight": temporal_weight}


def spatial_frame(frame, weights):
    padded = jnp.pad(frame.astype(jnp.float32), ((1, 1), (1, 1), (0, 0)))
    total = jnp.zeros(frame.shape, jnp.float32)
    for a in range(3):
        for b in range(3):
            total = total + jnp.einsum('hwc,cd->hwd', padded[a:a + H, b:b + W], weights[a, b].astype(jnp.float32))
    return total.astype(jnp.bfloat16)

def reference(video, cotangent, spatial_weight, temporal_weight):
    frames = video.reshape(CLIPS * FRAMES, H, W, C)
    hidden = lax.map(lambda f: spatial_frame(f, spatial_weight), frames).reshape(video.shape)
    hid32 = hidden.astype(jnp.float32)
    sig = jax.nn.sigmoid(hid32)
    act = (hid32 * sig).astype(jnp.bfloat16)
    grad32 = cotangent.astype(jnp.float32)
    wt32 = temporal_weight.astype(jnp.float32)
    padded = jnp.pad(grad32, ((0, 0), (0, 2), (0, 0), (0, 0), (0, 0)))
    act_grad = jnp.zeros(hid32.shape, jnp.float32)
    for k in range(3):
        act_grad = act_grad + jnp.einsum('nthwd,cd->nthwc', padded[:, k:k + FRAMES], wt32[k])
    hidden_grad = (act_grad * sig * (1.0 + hid32 * (1.0 - sig))).astype(jnp.bfloat16)
    scale = 1.0 / jnp.sqrt(jnp.float32(CLIPS * FRAMES * H * W))
    act32 = act.astype(jnp.float32)
    taps = []
    for k in range(3):
        taps.append(jnp.einsum('nthwc,nthwd->cd', act32[:, :FRAMES - k], grad32[:, k:]))
    temporal_grad = jnp.concatenate(taps, axis=0) * scale
    sw32 = spatial_weight.astype(jnp.float32)

    def frame_back(carry, pair):
        frame, dh = pair
        dh32 = dh.astype(jnp.float32)
        xpad = jnp.pad(frame.astype(jnp.float32), ((1, 1), (1, 1), (0, 0)))
        dpad = jnp.pad(dh32, ((1, 1), (1, 1), (0, 0)))
        back = jnp.zeros(frame.shape, jnp.float32)
        parts = []
        for a in range(3):
            for b in range(3):
                back = back + jnp.einsum('hwd,cd->hwc', dpad[2 - a:2 - a + H, 2 - b:2 - b + W], sw32[a, b])
                parts.append(jnp.einsum('hwc,hwd->cd', xpad[a:a + H, b:b + W], dh32))
        return (carry + jnp.concatenate(parts, axis=0), back.astype(jnp.bfloat16))
    init = jnp.zeros((9 * C, C), jnp.float32)
    summed, backs = lax.scan(frame_back, init, (frames, hidden_grad.reshape(CLIPS * FRAMES, H, W, C)))
    video_grad = backs.reshape(video.shape)
    return (video_grad, summed * scale, temporal_grad)
```

```python
import functools

import jax
import jax.numpy as jnp
from jax import lax
from jax.experimental import pallas as pl
from jax.experimental.pallas import tpu as pltpu
from jax.sharding import PartitionSpec as P

BF16, F32 = jnp.bfloat16, jnp.float32
VM = pl.BlockSpec(memory_space=pltpu.VMEM)
SM = pl.BlockSpec(memory_space=pltpu.SMEM)


def dot(a, b):
    return jnp.dot(a, b, preferred_element_type=F32)


def dot_rt(a, b):
    return lax.dot_general(a, b, (((1,), (1,)), ((), ())), preferred_element_type=F32)


def dot_lt(a, b):
    return lax.dot_general(a, b, (((0,), (0,)), ((), ())), preferred_element_type=F32)


def call(kernel, name, outs, smem, flops, *args, scratch=()):
    nbytes = sum(a.size * a.dtype.itemsize for a in (*args, *outs))
    return pl.pallas_call(
        kernel,
        out_shape=outs,
        in_specs=[SM] * smem + [VM] * (len(args) - smem),
        out_specs=[VM] * len(outs),
        scratch_shapes=[pltpu.VMEM(shape, dtype) for shape, dtype in scratch],
        compiler_params=pltpu.CompilerParams(vmem_limit_bytes=40 * 2**20),
        cost_estimate=pl.CostEstimate(flops=flops, bytes_accessed=nbytes, transcendentals=0),
        name=name,
    )(*args)


def tile(i, size):
    return pl.ds(pl.multiple_of(i * size, size), size)


def side_shifts(rows, width):
    n, chans = rows.shape
    wide = rows.astype(F32)
    column = lax.rem(lax.broadcasted_iota(jnp.int32, (n, chans), 0), width)
    left = jnp.where(column == 0, 0.0, pltpu.roll(wide, 1, 0))
    right = jnp.where(column == width - 1, 0.0, pltpu.roll(wide, n - 1, 0))
    return left.astype(BF16), right.astype(BF16)


def put_cat(cat, where, first, mid, last):
    chans = mid.shape[1]
    cat[where, :chans] = first
    cat[where, chans : 2 * chans] = mid
    cat[where, 2 * chans :] = last


def silu_parts(v):
    v = v.astype(F32)
    sig = 1.0 / (1.0 + jnp.exp(-v))
    return (v * sig).astype(BF16), sig * (1.0 + v * (1.0 - sig))


def conv_rows(cat, weight, out, rows, step, width):
    def body(i, carry):
        start = i * step
        acc = dot(cat[pl.ds(pl.multiple_of(start, width), step)], weight[0])
        for a in (1, 2):
            acc += dot(cat[pl.ds(pl.multiple_of(start + a * width, width), step)], weight[a])
        out[pl.ds(pl.multiple_of(start, width), step)] = acc.astype(BF16)
        return carry

    lax.fori_loop(0, rows // step, body, 0)


def hidden_kernel(width, video, weight, hidden, cat):
    rows = video.shape[0]
    chans3 = cat.shape[1]
    cat[:width] = jnp.zeros((width, chans3), BF16)
    cat[rows + width :] = jnp.zeros((width, chans3), BF16)

    def build(i, carry):
        mid = video[tile(i, 2 * width)]
        left, right = side_shifts(mid, width)
        put_cat(cat, pl.ds(pl.multiple_of(i * 2 * width + width, width), 2 * width), left, mid, right)
        return carry

    lax.fori_loop(0, rows // (2 * width), build, 0)
    conv_rows(cat, weight, hidden, rows, rows // 2, width)


def add_taps(total, video, cat, first, last, base, height, width):
    chans = video.shape[1]
    for a in range(3):
        low, high = max(first, 1 - a), min(last, height + 1 - a)
        rows = video[(low + a - 1 - base) * width : (high + a - 1 - base) * width]
        part = dot_lt(rows, cat[(low - first) * width : (high - first) * width])
        for b in range(3):
            total[3 * a + b] += part[:, b * chans : (b + 1) * chans]


def local_kernel(height, width, core, video, hidden, cot, mate, tw, rest, spatial, temporal, act, cat):
    rows, chans = video.shape
    half = rows // 2
    step = 2 * width
    even = core[0] == 0
    tap1 = jnp.where(even, tw[1], jnp.zeros_like(tw[1]))

    def top(i, carry):
        act[tile(i, step)] = silu_parts(hidden[tile(i, step)])[0]
        return carry

    def bottom(i, carry):
        here = pl.ds(pl.multiple_of(half + i * step, width), step)
        act_rows, slope = silu_parts(hidden[here])
        act[here] = act_rows
        grad = dot_rt(cot[here], tw[0]) + dot_rt(mate[here], tap1)
        rest[tile(i, step)] = grad
        mid = (grad * slope).astype(BF16)
        left, right = side_shifts(mid, width)
        put_cat(cat, tile(i, step), right, mid, left)
        return carry

    lax.fori_loop(0, half // step, top, 0)
    lax.fori_loop(0, half // step, bottom, 0)
    spatial[...] = jnp.zeros_like(spatial)
    add_taps(spatial, video, cat, height // 2, height, 0, height, width)
    temporal[0] = dot_lt(act[...], cot[...])
    temporal[1] = jnp.where(even, dot_lt(act[...], mate[...]), 0.0)


def halo_kernel(
    height, width, core, video, hidden, cot, mate, near, far, above, sw, tw, spatial, temporal,
    hidden_grad, spatial_out, temporal_out, act, cat, wide, total, other,
):
    rows, chans = video.shape
    half = rows // 2
    step = 2 * width
    even = core[0] == 0
    zero = jnp.zeros_like(tw[1])
    tap1_even = jnp.where(even, tw[1], zero)
    tap1_odd = jnp.where(even, zero, tw[1])

    def own(i, carry):
        here = tile(i, step)
        act_rows, slope = silu_parts(hidden[here])
        act[here] = act_rows
        grad = dot_rt(cot[here], tw[0]) + dot_rt(mate[here], tap1_even)
        grad += dot_rt(near[here], tw[1]) + dot_rt(far[here], tw[2])
        mid = (grad * slope).astype(BF16)
        hidden_grad[here] = mid
        left, right = side_shifts(mid, width)
        put_cat(cat, here, right, mid, left)
        return carry

    lax.fori_loop(0, half // step, own, 0)
    total[...] = spatial[...]
    add_taps(total, video, cat, 0, height // 2, 0, height, width)
    temporal_out[:chans] = temporal[0].astype(BF16)
    tap1 = temporal[1] + dot_lt(act[...], near[...])
    tap2 = dot_lt(act[...], far[...])

    blocks = above.shape[0] // width

    def build(i, carry):
        here = tile(i, width)
        mid = above[here]
        left, right = side_shifts(mid, width)
        put_cat(wide, here, left, mid, right)
        return carry

    lax.fori_loop(0, blocks, build, 0)
    wide[blocks * width :] = jnp.zeros((width, wide.shape[1]), BF16)
    conv_rows(wide, sw, other, half, half, width)

    def remote(i, carry):
        here = tile(i, step)
        there = pl.ds(pl.multiple_of(half + i * step, width), step)
        act_rows, slope = silu_parts(other[here])
        act[here] = act_rows
        grad = dot_rt(cot[there], tw[2]) + dot_rt(mate[there], tap1_odd)
        mid = (grad * slope).astype(BF16)
        left, right = side_shifts(mid, width)
        put_cat(cat, here, right, mid, left)
        return carry

    lax.fori_loop(0, half // step, remote, 0)
    add_taps(total, above, cat, height // 2, height, height // 2 - 1, height, width)
    tap2 += dot_lt(act[...], cot[half:])
    tap1 += jnp.where(even, 0.0, dot_lt(act[...], mate[half:]))
    temporal_out[chans : 2 * chans] = tap1.astype(BF16)
    temporal_out[2 * chans :] = tap2.astype(BF16)
    for tap in range(9):
        spatial_out[tap * chans : (tap + 1) * chans] = total[tap].astype(BF16)


def back_kernel(width, top, hidden, rest, near, far, tw, sw, out, cat):
    half = top.shape[0]
    step = 2 * width
    chans3 = cat.shape[1]
    cat[:width] = jnp.zeros((width, chans3), BF16)
    cat[2 * half + width :] = jnp.zeros((width, chans3), BF16)

    def first(i, carry):
        mid = top[tile(i, step)]
        left, right = side_shifts(mid, width)
        put_cat(cat, pl.ds(pl.multiple_of(width + i * step, width), step), right, mid, left)
        return carry

    def second(i, carry):
        here = tile(i, step)
        slope = silu_parts(hidden[pl.ds(pl.multiple_of(half + i * step, width), step)])[1]
        grad = rest[here] + dot_rt(near[here], tw[1]) + dot_rt(far[here], tw[2])
        mid = (grad * slope).astype(BF16)
        left, right = side_shifts(mid, width)
        put_cat(cat, pl.ds(pl.multiple_of(half + width + i * step, width), step), right, mid, left)
        return carry

    lax.fori_loop(0, half // step, first, 0)
    lax.fori_loop(0, half // step, second, 0)
    conv_rows(cat, sw, out, 2 * half, half, width)


def peer(index, k, size):
    return index ^ k if size & (size - 1) == 0 else (index + k) % size


def reduce_grads(spatial, temporal):
    dp, seq = lax.axis_size("dp"), lax.axis_size("seq")
    levels = seq // 2
    chans = spatial.shape[1]
    q, s = lax.axis_index("dp"), lax.axis_index("seq")
    core, level = s % 2, s // 2
    parts = [g.reshape(levels, 2, dp, -1, chans) for g in (spatial, temporal)]
    split = parts[0].shape[3]
    both = jnp.concatenate(parts, axis=3)
    pick = functools.partial(lax.dynamic_index_in_dim, keepdims=False)
    swapped = lax.ppermute(pick(both, 1 - core, 1), "seq", [(i, i ^ 1) for i in range(seq)])
    mine = (pick(both, core, 1).astype(F32) + swapped.astype(F32)).astype(BF16)
    got = [
        lax.ppermute(pick(mine, peer(q, k, dp), 1), "dp", [(i, peer(i, k, dp)) for i in range(dp)])
        for k in range(1, dp)
    ]
    held = sum((g.astype(F32) for g in got), pick(mine, q, 1).astype(F32)).astype(BF16)
    got = [
        lax.ppermute(
            pick(held, peer(level, k, levels), 0),
            "seq",
            [(i, 2 * peer(i // 2, k, levels) + i % 2) for i in range(seq)],
        )
        for k in range(1, levels)
    ]
    final = sum((g.astype(F32) for g in got), pick(held, level, 0).astype(F32))
    small = final.astype(BF16)
    whole = jnp.zeros((dp, *small.shape), BF16)
    whole = lax.dynamic_update_index_in_dim(whole, small, q, 0)
    for k in range(1, dp):
        part = lax.ppermute(small, "dp", [(peer(i, k, dp), i) for i in range(dp)])
        whole = lax.dynamic_update_index_in_dim(whole, part, peer(q, k, dp), 0)
    whole = whole.astype(F32)
    return whole[:, :split].reshape(-1, chans), whole[:, split:].reshape(-1, chans)


def shards(video, cotangent, spatial_weight, temporal_weight):
    height, width, chans = (video.shape[2], video.shape[3], video.shape[4])
    rows = height * width
    half = rows // 2
    seq = lax.axis_size("seq")
    total_count = lax.axis_size("dp") * video.shape[0] * seq * rows
    scale = 1.0 / jnp.sqrt(jnp.float32(total_count))
    core = (lax.axis_index("seq") % 2).astype(jnp.int32).reshape(1)
    x = video.reshape(rows, chans)
    cot = cotangent.reshape(rows, chans)
    sw = spatial_weight.reshape(3, 3 * chans, chans)
    sw_back = jnp.transpose(spatial_weight[::-1], (0, 1, 3, 2)).reshape(3, 3 * chans, chans)
    down = [(i + 2, i) for i in range(seq - 2)]
    up = [(i, i + 2) for i in range(seq - 2)]
    across = [(i, i + 1) for i in range(0, seq, 2)]
    far_top = lax.ppermute(cot[:half], "seq", down)
    above = lax.ppermute(x[half - width :], "seq", up)
    mate = lax.ppermute(cot, "seq", [(i, i ^ 1) for i in range(seq)])
    far_bottom = lax.ppermute(cot[half:], "seq", down)
    near_top = lax.ppermute(far_top, "seq", across)
    near_bottom = lax.ppermute(far_bottom, "seq", across)

    def array(n, dtype, columns=chans):
        return jax.ShapeDtypeStruct((n, columns), dtype)

    mac = rows * chans * chans
    (hidden,) = call(
        functools.partial(hidden_kernel, width), "hidden", [array(rows, BF16)], 0, 18 * mac, x, sw,
        scratch=[((rows + 2 * width, 3 * chans), BF16)],
    )
    taps9 = jax.ShapeDtypeStruct((9, chans, chans), F32)
    taps2 = jax.ShapeDtypeStruct((2, chans, chans), F32)
    rest, spatial, temporal = call(
        functools.partial(local_kernel, height, width), "local", [array(half, F32), taps9, taps2], 1, 15 * mac,
        core, x, hidden, cot, mate, temporal_weight,
        scratch=[((rows, chans), BF16), ((half, 3 * chans), BF16)],
    )
    top, spatial, temporal = call(
        functools.partial(halo_kernel, height, width), "halo",
        [array(half, BF16), array(9 * chans, BF16), array(3 * chans, BF16)], 1, 38 * mac,
        core, x, hidden, cot, mate, near_top, far_top, above, sw, temporal_weight, spatial, temporal,
        scratch=[
            ((half, chans), BF16), ((half, 3 * chans), BF16), ((half + 2 * width, 3 * chans), BF16),
            (taps9.shape, F32), ((half, chans), BF16),
        ],
    )
    spatial, temporal = reduce_grads(spatial, temporal)
    (back,) = call(
        functools.partial(back_kernel, width), "back", [array(rows, BF16)], 0, 20 * mac,
        top, hidden, rest, near_bottom, far_bottom, temporal_weight, sw_back,
        scratch=[((rows + 2 * width, 3 * chans), BF16)],
    )
    return (back.reshape(video.shape), spatial * scale, temporal * scale)


def solution(mesh):
    placed = (P("dp", "seq", None, None, None), P("dp", "seq", None, None, None), P(), P())
    return jax.shard_map(
        shards,
        mesh=mesh,
        in_specs=placed,
        out_specs=(P("dp", "seq", None, None, None), P("seq", None), P("seq", None)),
        check_vma=False,
    )
```

```python
import functools

import jax
import jax.numpy as jnp
from jax import lax
from jax.experimental import pallas as pl
from jax.experimental.pallas import tpu as pltpu
from jax.sharding import PartitionSpec as P

BF16, F32 = jnp.bfloat16, jnp.float32
EDGE = 8
LIMIT, FULL = 24 * 2**20, 60 * 2**20
REMOTE = 6
SPARE = 45056


def dot(a, b):
    return jnp.dot(a, b, preferred_element_type=F32)


def dot_rt(a, b):
    return lax.dot_general(a, b, (((1,), (1,)), ((), ())), preferred_element_type=F32)


def dot_lt(a, b):
    return lax.dot_general(a, b, (((0,), (0,)), ((), ())), preferred_element_type=F32)


def like(dtype, *shape):
    return jax.ShapeDtypeStruct(shape, dtype)


SPACE = {
    "s": pl.BlockSpec(memory_space=pltpu.SMEM),
    "v": pl.BlockSpec(memory_space=pltpu.VMEM),
    "h": pl.BlockSpec(memory_space=pl.ANY),
}


def call(kernel, name, spaces, flops, args, outs, scratch=(), copies=1, after=(), alias=None, limit=LIMIT):
    nbytes = sum(a.size * a.dtype.itemsize for a in (*args, *outs))
    ins, results = spaces.split()
    n_in, n_out = len(args), len(outs)

    def body(*refs):
        rest = refs[n_in + len(after) :]
        kernel(*refs[:n_in], *rest[:n_out], *rest[n_out + 1 :])
        rest[n_out][...] = jnp.zeros(TOKEN.shape, TOKEN.dtype)

    return pl.pallas_call(
        body,
        out_shape=[*outs, TOKEN],
        in_specs=[SPACE[c] for c in ins] + [SPACE["v"]] * len(after),
        out_specs=[SPACE[c] for c in results] + [SPACE["v"]],
        scratch_shapes=[*(pltpu.VMEM(s.shape, s.dtype) for s in scratch), pltpu.SemaphoreType.DMA((copies,))],
        input_output_aliases={} if alias is None else alias,
        compiler_params=pltpu.CompilerParams(vmem_limit_bytes=limit),
        cost_estimate=pl.CostEstimate(flops=flops, bytes_accessed=nbytes, transcendentals=0),
        name=name,
    )(*args, *after)


def start_all(sems, pairs, first=0):
    copies = [pltpu.make_async_copy(a, b, sems.at[first + i]) for i, (a, b) in enumerate(pairs)]
    for c in copies:
        c.start()
    return copies


def wait_all(copies):
    for c in copies:
        c.wait()


def behind(value, token):
    return lax.optimization_barrier((value, token))


TOKEN = like(F32, 8, 128)


def tile(i, size, base=0):
    return pl.ds(pl.multiple_of(base + i * size, size), size)


def loop(steps, body):
    def step(i, carry):
        body(i)
        return carry

    lax.fori_loop(0, steps, step, 0)


def silu_parts(v):
    v = v.astype(F32)
    sig = 0.5 * jnp.tanh(0.5 * v) + 0.5
    act = v * sig
    return act.astype(BF16), sig + act * (1.0 - sig)


def clear_edges(pad):
    n, long, chans = pad.shape
    pad[:, :EDGE] = jnp.zeros((n, EDGE, chans), F32)
    pad[:, long - EDGE :] = jnp.zeros((n, EDGE, chans), F32)


def put_shifts(cat, where, mid, pad):
    n, long, chans = pad.shape
    width = long - 2 * EDGE
    pad[:, EDGE : EDGE + width] = mid.astype(F32).reshape(n, width, chans)
    cat[where, chans : 2 * chans] = mid
    cat[where, :chans] = pad[:, EDGE + 1 : EDGE + 1 + width].astype(BF16).reshape(n * width, chans)
    cat[where, 2 * chans :] = pad[:, EDGE - 1 : EDGE - 1 + width].astype(BF16).reshape(n * width, chans)


def conv_rows(rows3, tap, out, step, wide, at=0):
    _, n, long, chans = wide.shape
    width = long - 2 * EDGE
    for side in range(2):
        clear_edges(wide.at[side])

    def body(i):
        start = i * step
        rows = [rows3[pl.ds(pl.multiple_of(start + a * width, width), step)] for a in range(3)]
        rows = jnp.concatenate(rows, axis=1)
        wide[0, :, EDGE : EDGE + width] = tap(rows, 0).reshape(n, width, chans)
        wide[1, :, EDGE : EDGE + width] = tap(rows, 2).reshape(n, width, chans)
        mid = tap(rows, 1).reshape(n, width, chans)
        mid += wide[0, :, EDGE - 1 : EDGE - 1 + width] + wide[1, :, EDGE + 1 : EDGE + 1 + width]
        out[tile(i, step, at)] = mid.reshape(step, chans).astype(BF16)

    loop((rows3.shape[0] - 2 * width) // step, body)


def forward_tap(sw):
    return lambda rows, b: dot(rows, jnp.concatenate([sw[a, b] for a in range(3)], axis=0))


def back_tap(sw):
    return lambda rows, b: dot_rt(rows, jnp.concatenate([sw[2 - a, 2 - b] for a in range(3)], axis=1))


def tap_parts(video, cat, first, last, base, height, width):
    chans = video.shape[1]
    for a in range(3):
        low, high = max(first, 1 - a), min(last, height + 1 - a)
        rows = video[(low + a - 1 - base) * width : (high + a - 1 - base) * width]
        part = dot_lt(rows, cat[(low - first) * width : (high - first) * width])
        for b in range(3):
            yield 3 * a + b, part[:, b * chans : (b + 1) * chans]


def cut_kernel(ranges, *refs):
    n = len(ranges)
    sources, targets, held, sems = refs[:n], refs[n : 2 * n], refs[2 * n : 3 * n], refs[-1]
    copies = start_all(sems, [(a.at[low:high], b) for a, b, (low, high) in zip(sources, held, ranges)])
    out = []
    for i, c in enumerate(copies):
        c.wait()
        out += start_all(sems, [(held[i], targets[i])], n + i)
    wait_all(out)


def local_kernel(
    height, width, upper, core, video, cot, mate, sw, tw, low, full, spatial, temporal,
    rows3, both, sw_v, tw_v, hidden_v, act, cat, wide, pad, rest, sems,
):
    rows, chans = video.shape
    step = 2 * width
    head = start_all(sems, [(video, rows3.at[width : rows + width]), (sw, sw_v)])
    tail = start_all(sems, [(cot, both.at[:, :chans]), (mate, both.at[:, chans:]), (tw, tw_v)], 2)
    rows3[:width] = jnp.zeros((width, chans), BF16)
    rows3[rows + width :] = jnp.zeros((width, chans), BF16)
    clear_edges(pad)
    wait_all(head)
    conv_rows(rows3, forward_tap(sw_v), hidden_v, wide.shape[1] * width, wide)
    out = start_all(sems, [(hidden_v, low.at[:rows])], 5)
    wait_all(tail)
    even = core[0] == 0
    tap0 = tw_v[0]
    tap1 = jnp.where(even, tw_v[1], jnp.zeros_like(tap0))
    taps = jnp.concatenate([tap0, tap1], axis=1)

    def top(i):
        here = tile(i, step)
        act[here] = silu_parts(hidden_v[here])[0]
        rest[here] = dot_rt(both[here], taps)

    def bottom(i):
        here = tile(i, step, upper * width)
        act_rows, slope = silu_parts(hidden_v[here])
        act[here] = act_rows
        grad = dot_rt(both[here], taps)
        rest[here] = grad
        put_shifts(cat, tile(i, step), (grad * slope).astype(BF16), pad)

    loop((height - upper) // 2, bottom)
    loop(upper // 2, top)
    out += start_all(sems, [(rest, full.at[:rows])], 6)
    for tap, part in tap_parts(rows3, cat, upper, height, -1, height, width):
        spatial[tap] = part
    part = dot_lt(act[...], both[...])
    temporal[0] = part[:, :chans]
    temporal[1] = jnp.where(even, part[:, chans:], 0.0)
    temporal[2] = jnp.zeros((chans, chans), F32)
    wait_all(out)


def remote_kernel(
    height, width, upper, core, above, cot, mate, sw, tw, spatial, temporal, spatial_out, temporal_out,
    rows3, both, sw_v, tw_v, other, act, cat, wide, pad, sems,
):
    chans = cot.shape[1]
    step = 2 * width
    at = upper * width
    held = above.shape[0]
    head = start_all(sems, [(above, rows3.at[:held]), (sw, sw_v)])
    tail = start_all(sems, [(mate.at[at:], both.at[:, :chans]), (cot.at[at:], both.at[:, chans:]), (tw, tw_v)], 2)
    even = core[0] == 0
    clear_edges(pad)
    rows3[held:] = jnp.zeros((width, chans), BF16)
    wait_all(head)
    conv_rows(rows3, forward_tap(sw_v), other, wide.shape[1] * width, wide)
    wait_all(tail)
    tap2 = tw_v[2]
    taps = jnp.concatenate([jnp.where(even, jnp.zeros_like(tap2), tw_v[1]), tap2], axis=1)

    def remote(i):
        here = tile(i, step)
        act_rows, slope = silu_parts(other[here])
        act[here] = act_rows
        grad = dot_rt(both[here], taps)
        put_shifts(cat, here, (grad * slope).astype(BF16), pad)

    loop((height - upper) // 2, remote)
    for tap, part in tap_parts(rows3, cat, upper, height, upper - 1, height, width):
        spatial_out[tap] = spatial[tap] + part
    part = dot_lt(act[...], both[...])
    temporal_out[0] = temporal[0]
    temporal_out[1] = temporal[1] + jnp.where(even, 0.0, part[:, :chans])
    temporal_out[2] = temporal[2] + part[:, chans:]


def last_kernel(
    height, width, upper, plan, core, video, near, far, tw, spatial, temporal, low_in, full_in,
    low, full, send, *scratch,
):
    rows, both, tw_v, hidden_v, rest, grad_v, act, cat, pad, total, total_t, *blocks, sems = scratch
    step = 2 * width
    chans = video.shape[1]
    count = upper * width
    whole = height * width
    head = start_all(
        sems, [(near, both.at[:, :chans]), (far, both.at[:, chans:]), (tw, tw_v), (low_in.at[:count], hidden_v), (full_in.at[:count], rest)]
    )
    tail = start_all(sems, [(video.at[: count + width], rows)], 5)
    clear_edges(pad)
    wait_all(head)
    taps = jnp.concatenate([tw_v[1], tw_v[2]], axis=1)

    def own(i):
        here = tile(i, step)
        act_rows, slope = silu_parts(hidden_v[here])
        act[here] = act_rows
        grad = rest[here] + dot_rt(both[here], taps)
        mid = (grad * slope).astype(BF16)
        grad_v[here] = mid
        put_shifts(cat, here, mid, pad)

    loop(upper // 2, own)
    out = start_all(sems, [(grad_v, low.at[whole : whole + count])], 6)
    wait_all(tail)
    for tap, part in tap_parts(rows, cat, 0, upper, 0, height, width):
        total[tap * chans : (tap + 1) * chans] = spatial[tap] + part
    part = dot_lt(act[...], both[...])
    total_t[:chans] = temporal[0]
    total_t[chans : 2 * chans] = temporal[1] + part[:, :chans]
    total_t[2 * chans :] = temporal[2] + part[:, chans:]
    if plan is None:
        n = total.shape[0]
        out += start_all(sems, [(total, full.at[whole : whole + n]), (total_t, full.at[whole + n : whole + n + total_t.shape[0]])], 7)
        wait_all(out)
        return
    keep_v, send_v = blocks
    dp, levels, rs, rt = plan

    def block(at, i):
        return jnp.concatenate(
            [
                total[pl.ds(pl.multiple_of((at * dp + i) * rs, 8), rs)],
                total_t[pl.ds(pl.multiple_of((at * dp + i) * rt, 8), rt)],
            ],
            axis=0,
        )

    size = rs + rt
    for level in range(levels):
        for i in range(dp):
            send_v[i, level] = block(2 * level + 1 - core[0], i).astype(BF16)
    out += start_all(sems, [(send_v, send)], 7)
    for i in range(dp):
        for level in range(levels):
            at = (i * levels + level) * size
            keep_v[at : at + size] = block(2 * level + core[0], i)
    n = keep_v.shape[0]
    wait_all(out + start_all(sems, [(keep_v, full.at[whole : whole + n])], 8))


def back_top_kernel(whole, width, low, sw, back, rows3, sw_v, out, wide, sems):
    chans = out.shape[1]
    held = rows3.shape[0] - width
    head = start_all(sems, [(low.at[whole : whole + held], rows3.at[width:]), (sw, sw_v)])
    rows3[:width] = jnp.zeros((width, chans), BF16)
    wait_all(head)
    conv_rows(rows3, back_tap(sw_v), out, wide.shape[1] * width, wide)
    wait_all(start_all(sems, [(out, back.at[: out.shape[0]])], 2))


def back_bottom_kernel(
    whole, width, upper, low, full, near, far, tw, sw, _, back,
    rows3, both, hidden_v, rest, tw_v, sw_v, out, wide, sems,
):
    chans = out.shape[1]
    step = 2 * width
    count = near.shape[0]
    first = upper * width
    top = rows3.shape[0] - width - count
    head = start_all(
        sems,
        [
            (near, both.at[:, :chans]), (far, both.at[:, chans:]), (tw, tw_v), (low.at[first:whole], hidden_v),
            (full.at[first:whole], rest), (low.at[whole + first - top : whole + first], rows3.at[:top]), (sw, sw_v),
        ],
    )
    rows3[rows3.shape[0] - width :] = jnp.zeros((width, chans), BF16)
    wait_all(head)
    taps = jnp.concatenate([tw_v[1], tw_v[2]], axis=1)

    def rest_rows(i):
        here = tile(i, step)
        slope = silu_parts(hidden_v[here])[1]
        grad = rest[here] + dot_rt(both[here], taps)
        rows3[pl.ds(pl.multiple_of(top + i * step, width), step)] = (grad * slope).astype(BF16)

    loop(count // step, rest_rows)
    conv_rows(rows3, back_tap(sw_v), out, wide.shape[1] * width, wide)
    wait_all(start_all(sems, [(out, back.at[back.shape[0] - out.shape[0] :])], 7))


def peer(index, k, size):
    return index ^ k if size & (size - 1) == 0 else (index + k) % size


def split_kernel(size, first, where, kept, swapped, own, *refs):
    sends, (keep_v, swapped_v, own_v, send_v, sems) = refs[: size - 1], refs[size - 1 :]
    q = where[0]
    levels, each = own.shape[:2]
    n = keep_v.shape[0]
    wait_all(start_all(sems, [(kept.at[first : first + n], keep_v), (swapped, swapped_v)]))

    def total(i):
        mine = keep_v[pl.ds(pl.multiple_of(i * levels * each, 8), levels * each)]
        return mine.reshape(own.shape) + swapped_v[i].astype(F32)

    out = []
    for k, send in enumerate(sends):
        send_v[k] = total(peer(q, k + 1, size)).astype(BF16)
        out += start_all(sems, [(send_v.at[k], send)], 2 + k)
    own_v[...] = total(q)
    wait_all(out + start_all(sems, [(own_v, own)], 1 + size))


def level_kernel(size, where, own, *refs):
    got = refs[: -size - 3]
    mine, *sends = refs[-size - 3 : -3]
    own_v, got_v, sems = refs[-3:]
    level = where[0]
    wait_all(start_all(sems, [(own, own_v), *((g, got_v.at[k]) for k, g in enumerate(got))]))

    def total(i):
        return sum((got_v[k, i].astype(F32) for k in range(len(got))), own_v[i])

    mine[...] = total(level)
    for k, out in enumerate(sends, 1):
        out[...] = total(peer(level, k, size)).astype(BF16)


def sum_kernel(own, *refs):
    *got, out, _ = refs
    out[...] = sum((g[...].astype(F32) for g in got), own[...]).astype(BF16)


def place_kernel(scale, where, small, *refs):
    *got, spatial, temporal, _ = refs
    size, rs, rt = len(got) + 1, spatial.shape[1], temporal.shape[1]
    for k, part in enumerate((small, *got)):
        at = peer(where[0], k, size)
        rows = part[...].astype(F32) * scale
        spatial[at] = rows[:rs]
        temporal[at] = rows[rs:]


def shards(video, cotangent, spatial_weight, temporal_weight):
    height, width, chans = (video.shape[2], video.shape[3], video.shape[4])
    rows = height * width
    dp, seq = lax.axis_size("dp"), lax.axis_size("seq")
    levels = seq // 2
    scale = float((dp * video.shape[0] * seq * rows) ** -0.5)
    dp_at, seq_at = lax.axis_index("dp").astype(jnp.int32), lax.axis_index("seq").astype(jnp.int32)
    core, level, q = (v.reshape(1) for v in (seq_at % 2, seq_at // 2, dp_at))
    x = video.reshape(rows, chans)
    cot = cotangent.reshape(rows, chans)
    sw, tw = spatial_weight, temporal_weight
    upper = height - REMOTE
    whole = rows
    down = [(i + 2, i) for i in range(seq - 2)]
    up = [(i, i + 2) for i in range(seq - 2)]
    across = [(i, i + 1) for i in range(0, seq, 2)]
    swap = [(i, i ^ 1) for i in range(seq)]

    mac = rows * chans * chans
    long = width + 2 * EDGE
    pad = like(F32, 2, long, chans)
    taps9, taps3 = (like(F32, n, chans, chans) for n in (9, 3))

    def rows_of(n, columns=chans, dtype=BF16):
        return like(dtype, n * width, columns)

    def wide(n):
        return like(F32, 2, n, long, chans)

    mate = lax.ppermute(cot, "seq", swap)
    ranges = [((upper - 1) * width, rows), (0, upper * width), (upper * width, rows)]
    slices = [like(BF16, high - low, chans) for low, high in ranges]
    *slices, token = call(
        functools.partial(cut_kernel, ranges), "cut", "hhh hhh", 0, [x, cot, cot], slices, slices, copies=6, limit=FULL
    )
    above = lax.ppermute(slices[0], "seq", up)
    far = lax.ppermute(slices[1], "seq", down)
    far3 = lax.ppermute(slices[2], "seq", down)
    low, full, spatial, temporal, token = call(
        functools.partial(local_kernel, height, width, upper), "local", "shhhhh hhvv", 34 * mac,
        [core, x, cot, mate, sw, tw], [like(BF16, 2 * SPARE, chans), like(F32, SPARE, chans), taps9, taps3],
        [
            rows_of(height + 2), rows_of(height, 2 * chans), sw, tw, rows_of(height), rows_of(height),
            rows_of(REMOTE, 3 * chans), wide(height // 2), pad, rows_of(height, dtype=F32),
        ],
        copies=7,
    )
    spatial, temporal, token = call(
        functools.partial(remote_kernel, height, width, upper), "remote", "shhhhhvv vv", 16 * mac,
        [core, above, cot, mate, sw, tw, spatial, temporal], [taps9, taps3],
        [
            rows_of(REMOTE + 2), rows_of(REMOTE, 2 * chans), sw, tw, rows_of(REMOTE), rows_of(REMOTE),
            rows_of(REMOTE, 3 * chans), wide(REMOTE), pad,
        ],
        copies=5, after=[token],
    )

    far, token = behind(far, token)
    near = lax.ppermute(far, "seq", across)
    rs, rt = 9 * chans // (seq * dp), 3 * chans // (seq * dp)
    plain = rs % 8 or rt % 8 or (rs + rt) % 16
    flat = [like(F32, 9 * chans, chans), like(F32, 3 * chans, chans)]
    send = like(BF16, dp, levels, rs + rt, chans)
    blocks = [] if plain else [like(F32, 12 * chans // 2, chans), send]
    low, full, send, token = call(
        functools.partial(last_kernel, height, width, upper, None if plain else (dp, levels, rs, rt)), "last", "shhhhvvhh hhh", 16 * mac,
        [core, x, near, far, tw, spatial, temporal, low, full], [low, full, send],
        [
            rows_of(upper + 1), rows_of(upper, 2 * chans), tw, rows_of(upper), rows_of(upper, dtype=F32), rows_of(upper),
            rows_of(upper), rows_of(upper, 3 * chans), pad, *flat, *blocks,
        ],
        copies=9, after=[token], alias={7: 0, 8: 1},
    )
    kept, first = full, whole
    if plain:
        parts = (full[whole : whole + 9 * chans], full[whole + 9 * chans : whole + 12 * chans])
        both = jnp.concatenate([g.reshape(levels, 2, dp, -1, chans) for g in parts], axis=3)
        both = jnp.transpose(both, (1, 2, 0, 3, 4))
        kept, first = lax.dynamic_index_in_dim(both, core[0], 0, keepdims=False).reshape(-1, chans), 0
        send = lax.dynamic_index_in_dim(both, 1 - core[0], 0, keepdims=False).astype(BF16)

    got = lax.ppermute(send, "seq", swap)
    piece = (levels, rs + rt, chans)
    own, *sends, token = call(
        functools.partial(split_kernel, dp, first), "split", "shh " + "h" * dp, mac // 8, [q, kept, got],
        [like(F32, *piece)] + [like(BF16, *piece)] * (dp - 1),
        [like(F32, 12 * chans // 2, chans), send, like(F32, *piece), like(BF16, dp - 1, *piece)], copies=dp + 2,
    )
    got = [lax.ppermute(s, "dp", [(i, peer(i, k, dp)) for i in range(dp)]) for k, s in enumerate(sends, 1)]
    back, token = call(
        functools.partial(back_top_kernel, whole, width), "back_top", "hh h", 9 * mac, [low, sw], [rows_of(height)],
        [rows_of(height // 2 + 2), sw, rows_of(height // 2), wide(height // 2)], copies=3, after=[token],
    )
    level_piece = (rs + rt, chans)
    own, *sends, token = call(
        functools.partial(level_kernel, levels), "level", "sh" + "h" * (dp - 1) + " " + "v" * levels, mac // 8,
        [level, own, *got], [like(F32, *level_piece)] + [like(BF16, *level_piece)] * (levels - 1),
        [like(F32, *piece), like(BF16, dp - 1, *piece)], copies=dp, after=[token],
    )
    far3, token = behind(far3, token)
    near3 = lax.ppermute(far3, "seq", across)
    got = [
        lax.ppermute(s, "seq", [(i, 2 * peer(i // 2, k, levels) + i % 2) for i in range(seq)])
        for k, s in enumerate(sends, 1)
    ]
    back, token = call(
        functools.partial(back_bottom_kernel, whole, width, upper), "back_bottom", "hhhhhhh h", 12 * mac,
        [low, full, near3, far3, tw, sw, back], [rows_of(height)],
        [
            rows_of(height // 2 + 2), rows_of(REMOTE, 2 * chans), rows_of(REMOTE), rows_of(REMOTE, dtype=F32),
            tw, sw, rows_of(height // 2), wide(height // 2),
        ],
        copies=8, after=[token], alias={6: 0},
    )
    small, token = call(
        sum_kernel, "sum", "v" * levels + " v", mac // 8, [own, *got], [like(BF16, *level_piece)], after=[token]
    )
    got = [lax.ppermute(small, "dp", [(peer(i, k, dp), i) for i in range(dp)]) for k in range(1, dp)]
    spatial, temporal, token = call(
        functools.partial(place_kernel, scale), "place", "s" + "v" * dp + " vv", mac // 8, [q, small, *got],
        [like(F32, dp, rs, chans), like(F32, dp, rt, chans)],
    )
    return (back.reshape(video.shape), spatial.reshape(-1, chans), temporal.reshape(-1, chans))


def solution(mesh):
    placed = (P("dp", "seq", None, None, None), P("dp", "seq", None, None, None), P(), P())
    return jax.shard_map(
        shards,
        mesh=mesh,
        in_specs=placed,
        out_specs=(P("dp", "seq", None, None, None), P("seq", None), P("seq", None)),
        check_vma=False,
    )
```

```python
import functools

import jax
import jax.numpy as jnp
from jax import lax
from jax.experimental import pallas as pl
from jax.experimental.pallas import tpu as pltpu
from jax.sharding import PartitionSpec as P

BF16, F32 = jnp.bfloat16, jnp.float32
EDGE = 8
LIMIT, FULL = 24 * 2**20, 60 * 2**20
REMOTE = 6
SPARE = 45056


def dot(a, b):
    return jnp.dot(a, b, preferred_element_type=F32)


def dot_rt(a, b):
    return lax.dot_general(a, b, (((1,), (1,)), ((), ())), preferred_element_type=F32)


def dot_lt(a, b):
    return lax.dot_general(a, b, (((0,), (0,)), ((), ())), preferred_element_type=F32)


def like(dtype, *shape):
    return jax.ShapeDtypeStruct(shape, dtype)


SPACE = {
    "s": pl.BlockSpec(memory_space=pltpu.SMEM),
    "v": pl.BlockSpec(memory_space=pltpu.VMEM),
    "h": pl.BlockSpec(memory_space=pl.ANY),
}


def call(kernel, name, spaces, flops, args, outs, scratch=(), copies=0, after=(), alias=None, limit=LIMIT):
    nbytes = sum(a.size * a.dtype.itemsize for a in (*args, *outs) if a.shape[0] < SPARE)
    ins, results = spaces.split()
    n_in, n_out = len(args), len(outs)

    def body(*refs):
        rest = refs[n_in + len(after) :]
        kernel(*refs[:n_in], *rest[:n_out], *rest[n_out + 1 :])
        rest[n_out][...] = jnp.zeros(TOKEN.shape, TOKEN.dtype)

    return pl.pallas_call(
        body,
        out_shape=[*outs, TOKEN],
        in_specs=[SPACE[c] for c in ins] + [SPACE["v"]] * len(after),
        out_specs=[SPACE[c] for c in results] + [SPACE["v"]],
        scratch_shapes=[*(pltpu.VMEM(s.shape, s.dtype) for s in scratch), *([pltpu.SemaphoreType.DMA((copies,))] if copies else [])],
        input_output_aliases={} if alias is None else alias,
        compiler_params=pltpu.CompilerParams(vmem_limit_bytes=limit),
        cost_estimate=pl.CostEstimate(flops=flops, bytes_accessed=nbytes, transcendentals=0),
        name=name,
    )(*args, *after)


class Copies:
    def __init__(self, sems):
        self.sems, self.used = sems, 0

    def start(self, *pairs):
        started = []
        for a, b in pairs:
            started.append(pltpu.make_async_copy(a, b, self.sems.at[self.used]))
            self.used += 1
            started[-1].start()
        return started


def wait_all(copies):
    for c in copies:
        c.wait()


def behind(value, token):
    return lax.optimization_barrier((value, token))


TOKEN = like(F32, 8, 128)


def tile(i, size, base=0):
    return pl.ds(pl.multiple_of(base + i * size, size), size)


def loop(steps, body):
    def step(i, carry):
        body(i)
        return carry

    lax.fori_loop(0, steps, step, 0)


def silu_parts(v):
    v = v.astype(F32)
    sig = 0.5 * jnp.tanh(0.5 * v) + 0.5
    act = v * sig
    return act.astype(BF16), sig + act * (1.0 - sig)


def clear_edges(pad):
    n, long, chans = pad.shape
    pad[:, :EDGE] = jnp.zeros((n, EDGE, chans), F32)
    pad[:, long - EDGE :] = jnp.zeros((n, EDGE, chans), F32)


def put_shifts(cat, where, mid, pad):
    n, long, chans = pad.shape
    width = long - 2 * EDGE
    pad[:, EDGE : EDGE + width] = mid.astype(F32).reshape(n, width, chans)
    cat[where, chans : 2 * chans] = mid
    cat[where, :chans] = pad[:, EDGE + 1 : EDGE + 1 + width].astype(BF16).reshape(n * width, chans)
    cat[where, 2 * chans :] = pad[:, EDGE - 1 : EDGE - 1 + width].astype(BF16).reshape(n * width, chans)


def conv_rows(rows3, tap, out, step, wide, at=0):
    _, n, long, chans = wide.shape
    width = long - 2 * EDGE
    for side in range(2):
        clear_edges(wide.at[side])

    def body(i):
        start = i * step
        rows = [rows3[pl.ds(pl.multiple_of(start + a * width, width), step)] for a in range(3)]
        rows = jnp.concatenate(rows, axis=1)
        wide[0, :, EDGE : EDGE + width] = tap(rows, 0).reshape(n, width, chans)
        wide[1, :, EDGE : EDGE + width] = tap(rows, 2).reshape(n, width, chans)
        mid = tap(rows, 1).reshape(n, width, chans)
        mid += wide[0, :, EDGE - 1 : EDGE - 1 + width] + wide[1, :, EDGE + 1 : EDGE + 1 + width]
        out[tile(i, step, at)] = mid.reshape(step, chans).astype(BF16)

    loop((rows3.shape[0] - 2 * width) // step, body)


def forward_tap(sw):
    return lambda rows, b: dot(rows, jnp.concatenate([sw[a, b] for a in range(3)], axis=0))


def back_tap(sw):
    return lambda rows, b: dot_rt(rows, jnp.concatenate([sw[2 - a, 2 - b] for a in range(3)], axis=1))


def tap_parts(video, cat, first, last, base, height, width):
    chans = video.shape[1]
    for a in range(3):
        low, high = max(first, 1 - a), min(last, height + 1 - a)
        rows = video[(low + a - 1 - base) * width : (high + a - 1 - base) * width]
        part = dot_lt(rows, cat[(low - first) * width : (high - first) * width])
        for b in range(3):
            yield 3 * a + b, part[:, b * chans : (b + 1) * chans]


def local_kernel(
    height, width, upper, core, video, cot, mate, sw, tw, hidden_top, rest, spatial, temporal, low,
    rows3, both, sw_v, tw_v, hidden_v, act, cat, wide, pad, grad_v, sems,
):
    rows, chans = video.shape
    top_rows = upper * width
    copies = Copies(sems)
    head = copies.start((video, rows3.at[width : rows + width]), (sw, sw_v))
    tail = copies.start((cot, both.at[:, :chans]), (mate, both.at[:, chans:]), (tw, tw_v))
    rows3[:width] = jnp.zeros((width, chans), BF16)
    rows3[rows + width :] = jnp.zeros((width, chans), BF16)
    clear_edges(pad)
    wait_all(head)
    conv_rows(rows3, forward_tap(sw_v), hidden_v, wide.shape[1] * width, wide)
    wait_all(tail)
    even = core[0] == 0
    tap0 = tw_v[0]
    tap1 = jnp.where(even, tw_v[1], jnp.zeros_like(tap0))
    taps = jnp.concatenate([tap0, tap1], axis=1)
    step = pad.shape[0] * width

    def bottom(i):
        here = pl.ds(pl.multiple_of(top_rows + i * step, width), step)
        act_rows, slope = silu_parts(hidden_v[here])
        act[here] = act_rows
        mid = (dot_rt(both[here], taps) * slope).astype(BF16)
        grad_v[tile(i, step)] = mid
        put_shifts(cat, tile(i, step), mid, pad)

    loop((rows - top_rows) // step, bottom)
    out = copies.start((grad_v, low.at[rows + top_rows : 2 * rows]))
    top_step = top_rows // 2

    def top(i):
        here = tile(i, top_step)
        v = hidden_v[here]
        hidden_top[here] = v
        act[here] = silu_parts(v)[0]
        rest[here] = dot_rt(both[here], taps)

    loop(2, top)
    for tap, part in tap_parts(rows3, cat, upper, height, -1, height, width):
        spatial[tap] = part
    part = dot_lt(act[...], both[...])
    temporal[0] = part[:, :chans]
    temporal[1] = jnp.where(even, part[:, chans:], 0.0)
    temporal[2] = jnp.zeros((chans, chans), F32)
    wait_all(out)


def remote_kernel(
    height, width, upper, core, above, cot, mate, sw, tw, spatial, temporal, spatial_out, temporal_out, grad,
    rows3, both, sw_v, tw_v, other, act, cat, wide, pad, grad_v, sems,
):
    chans = cot.shape[1]
    at = upper * width
    held = above.shape[0]
    copies = Copies(sems)
    head = copies.start((above, rows3.at[:held]), (sw, sw_v))
    tail = copies.start((mate.at[at:], both.at[:, :chans]), (cot.at[at:], both.at[:, chans:]), (tw, tw_v))
    even = core[0] == 0
    clear_edges(pad)
    rows3[held:] = jnp.zeros((width, chans), BF16)
    wait_all(head)
    conv_rows(rows3, forward_tap(sw_v), other, wide.shape[1] * width, wide)
    wait_all(tail)
    tap2 = tw_v[2]
    taps = jnp.concatenate([jnp.where(even, jnp.zeros_like(tap2), tw_v[1]), tap2], axis=1)
    step = pad.shape[0] * width

    def remote(i):
        here = tile(i, step)
        act_rows, slope = silu_parts(other[here])
        act[here] = act_rows
        mid = (dot_rt(both[here], taps) * slope).astype(BF16)
        grad_v[here] = mid
        put_shifts(cat, here, mid, pad)

    loop((height - upper) * width // step, remote)
    out = copies.start((grad_v, grad))
    for tap, part in tap_parts(rows3, cat, upper, height, upper - 1, height, width):
        spatial_out[tap] = spatial[tap] + part
    part = dot_lt(act[...], both[...])
    temporal_out[0] = temporal[0]
    temporal_out[1] = temporal[1] + jnp.where(even, 0.0, part[:, :chans])
    temporal_out[2] = temporal[2] + part[:, chans:]
    wait_all(out)


def own_kernel(
    height, width, upper, plain, core, video, hidden, rest, near, far, tw, spatial, temporal, low_in, low, full, send,
    rows, both, tw_v, act, cat, pad, grad_v, total, total_t, send_v, sems,
):
    count, chans = near.shape
    whole = height * width
    copies = Copies(sems)
    head = copies.start((near, both.at[:, :chans]), (far, both.at[:, chans:]), (tw, tw_v))
    tail = copies.start((video.at[: count + width], rows))
    clear_edges(pad)
    wait_all(head)
    taps = jnp.concatenate([tw_v[1], tw_v[2]], axis=1)
    step = pad.shape[0] * width

    def own(i):
        here = tile(i, step)
        act_rows, slope = silu_parts(hidden[here])
        act[here] = act_rows
        grad = rest[here] + dot_rt(both[here], taps)
        mid = (grad * slope).astype(BF16)
        grad_v[here] = mid
        put_shifts(cat, here, mid, pad)

    loop(count // step, own)
    out = copies.start((grad_v, low.at[whole : whole + count]))
    part = dot_lt(act[...], both[...])
    total_t[:chans] = temporal[0]
    total_t[chans : 2 * chans] = temporal[1] + part[:, :chans]
    total_t[2 * chans :] = temporal[2] + part[:, chans:]
    n, first = total.shape[0], 0
    out += copies.start((total_t, full.at[n : n + total_t.shape[0]]))
    wait_all(tail)
    levels, each = send.shape[:2]
    rt = total_t.shape[0] // (2 * levels)
    rs = each - rt
    for tap, part in tap_parts(rows, cat, 0, upper, 0, height, width):
        total[tap * chans : (tap + 1) * chans] = spatial[tap] + part
        if tap % 3 == 2:
            at = (tap - 2) * chans
            out += copies.start((total.at[at : at + 3 * chans], full.at[at : at + 3 * chans]))
        if plain:
            continue
        while first < levels and (first + 1) * 2 * rs <= (tap + 1) * chans:
            at = 2 * first + 1 - core[0]
            send_v[first, :rs] = total[pl.ds(pl.multiple_of(at * rs, 8), rs)].astype(BF16)
            send_v[first, rs:] = total_t[pl.ds(pl.multiple_of(at * rt, 8), rt)].astype(BF16)
            out += copies.start((send_v.at[first], send.at[first]))
            first += 1
    wait_all(out)


def back_top_kernel(whole, width, low, sw, back, rows3, sw_v, out, wide, sems):
    chans = out.shape[1]
    held = rows3.shape[0] - width
    copies = Copies(sems)
    head = copies.start((low.at[whole : whole + held], rows3.at[width:]), (sw, sw_v))
    rows3[:width] = jnp.zeros((width, chans), BF16)
    wait_all(head)
    conv_rows(rows3, back_tap(sw_v), out, wide.shape[1] * width, wide)
    wait_all(copies.start((out, back.at[: out.shape[0]])))


def back_bottom_kernel(whole, width, low, got, sw, _, back, rows3, got_v, sw_v, out, wide, sems):
    chans = out.shape[1]
    held = rows3.shape[0] - width
    count = got.shape[0]
    copies = Copies(sems)
    head = copies.start((low.at[2 * whole - held : 2 * whole], rows3.at[:held]), (sw, sw_v))
    head += copies.start((got, got_v))
    rows3[held:] = jnp.zeros((width, chans), BF16)
    wait_all(head)

    def add(i):
        here = pl.ds(pl.multiple_of(held - count + i * width, width), width)
        rows3[here] = (rows3[here].astype(F32) + got_v[tile(i, width)].astype(F32)).astype(BF16)

    loop(count // width, add)
    conv_rows(rows3, back_tap(sw_v), out, wide.shape[1] * width, wide)
    wait_all(copies.start((out, back.at[back.shape[0] - out.shape[0] :])))


def peer(index, k, size):
    return index ^ k if size & (size - 1) == 0 else (index + k) % size


def split_kernel(size, where, kept, swapped, own, *refs):
    sends, (keep_v, swapped_v, send_v, sems) = refs[: size - 1], refs[size - 1 :]
    core, q = where[0], where[1]
    levels, each, chans = swapped.shape
    rs = own.shape[1] * 3 // 4
    rt = own.shape[1] - rs
    copies = Copies(sems)
    pairs = [(swapped, swapped_v)]
    for level in range(levels):
        at = 2 * level + core
        low = pl.ds(pl.multiple_of(at * size * rs, 8), size * rs)
        high = pl.ds(pl.multiple_of(2 * levels * size * rs + at * size * rt, 8), size * rt)
        pairs += [(kept.at[low], keep_v.at[level, : size * rs]), (kept.at[high], keep_v.at[level, size * rs :])]
    ins = copies.start(*pairs)
    ins[0].wait()
    for level in range(levels):
        wait_all(ins[1 + 2 * level : 3 + 2 * level])
        keep_v[level] += swapped_v[level].astype(F32)

    def total(i, level):
        low = keep_v[level, pl.ds(pl.multiple_of(i * rs, 8), rs)]
        return jnp.concatenate([low, keep_v[level, pl.ds(pl.multiple_of(size * rs + i * rt, 8), rt)]], axis=0)

    out = []
    for k, send in enumerate(sends):
        for level in range(levels):
            send_v[k, level] = total(peer(q, k + 1, size), level).astype(BF16)
        out += copies.start((send_v.at[k], send))
    for level in range(levels):
        own[level] = total(q, level)
    wait_all(out)


def level_kernel(size, where, own, *refs):
    got = refs[: -size - 2]
    mine, *sends = refs[-size - 2 : -2]
    got_v, sems = refs[-2:]
    level = where[0]
    copies = Copies(sems)
    wait_all(copies.start(*((g, got_v.at[k]) for k, g in enumerate(got))))

    def total(i):
        return sum((got_v[k, i].astype(F32) for k in range(len(got))), own[i])

    mine[...] = total(level)
    for k, out in enumerate(sends, 1):
        out[...] = total(peer(level, k, size)).astype(BF16)


def sum_kernel(own, *refs):
    *got, out = refs
    out[...] = sum((g[...].astype(F32) for g in got), own[...]).astype(BF16)


def place_kernel(scale, where, small, *refs):
    *got, spatial, temporal = refs
    size, rs, rt = len(got) + 1, spatial.shape[1], temporal.shape[1]
    for k, part in enumerate((small, *got)):
        at = peer(where[0], k, size)
        rows = part[...].astype(F32) * scale
        spatial[at] = rows[:rs]
        temporal[at] = rows[rs:]


def shards(video, cotangent, spatial_weight, temporal_weight):
    height, width, chans = (video.shape[2], video.shape[3], video.shape[4])
    rows = height * width
    dp, seq = lax.axis_size("dp"), lax.axis_size("seq")
    levels = seq // 2
    scale = float((dp * video.shape[0] * seq * rows) ** -0.5)
    dp_at, seq_at = lax.axis_index("dp").astype(jnp.int32), lax.axis_index("seq").astype(jnp.int32)
    core, level, q = (v.reshape(1) for v in (seq_at % 2, seq_at // 2, dp_at))
    x = video.reshape(rows, chans)
    cot = cotangent.reshape(rows, chans)
    sw, tw = spatial_weight, temporal_weight
    upper = height - REMOTE
    down = [(i + 2, i) for i in range(seq - 2)]
    up = [(i, i + 2) for i in range(seq - 2)]
    across = [(i, i + 1) for i in range(0, seq, 2)]
    swap = [(i, i ^ 1) for i in range(seq)]

    mac = rows * chans * chans
    long = width + 2 * EDGE
    taps9, taps3 = (like(F32, n, chans, chans) for n in (9, 3))

    def rows_of(n, columns=chans, dtype=BF16):
        return like(dtype, n * width, columns)

    def wide(n):
        return like(F32, 2, n, long, chans)

    mate = lax.ppermute(cot, "seq", swap)
    far = lax.ppermute(cot[: upper * width], "seq", down)
    above = lax.ppermute(x[(upper - 1) * width :], "seq", up)

    def pad(n):
        return like(F32, n, long, chans)

    hidden, rest, spatial, temporal, low, token = call(
        functools.partial(local_kernel, height, width, upper), "local", "shhhhh vvvvh", 34 * mac, [core, x, cot, mate, sw, tw],
        [rows_of(upper), rows_of(upper, dtype=F32), taps9, taps3, like(BF16, 2 * SPARE, chans)],
        [
            rows_of(height + 2), rows_of(height, 2 * chans), sw, tw, rows_of(height), rows_of(height),
            rows_of(REMOTE, 3 * chans), wide(height // 2), pad(REMOTE), rows_of(REMOTE),
        ],
        copies=6,
    )
    far, token = behind(far, token)
    near = lax.ppermute(far, "seq", across)
    spatial, temporal, cross, token = call(
        functools.partial(remote_kernel, height, width, upper), "remote", "shhhhhvv vvh", 16 * mac,
        [core, above, cot, mate, sw, tw, spatial, temporal], [taps9, taps3, rows_of(REMOTE)],
        [
            rows_of(REMOTE + 2), rows_of(REMOTE, 2 * chans), sw, tw, rows_of(REMOTE), rows_of(REMOTE),
            rows_of(REMOTE, 3 * chans), wide(REMOTE), pad(REMOTE), rows_of(REMOTE),
        ],
        copies=6, after=[token],
    )
    rs, rt = 9 * chans // (seq * dp), 3 * chans // (seq * dp)
    plain = bool(rs % 8 or rt % 8 or dp * rs % 16 or dp * rt % 16)
    send = like(BF16, levels, dp * (rs + rt), chans)
    low, full, send, token = call(
        functools.partial(own_kernel, height, width, upper, plain), "own", "shvvhhhvvh hhh", 16 * mac,
        [core, x, hidden, rest, near, far, tw, spatial, temporal, low], [low, like(F32, SPARE, chans), send],
        [
            rows_of(upper + 1), rows_of(upper, 2 * chans), tw, rows_of(upper), rows_of(upper, 3 * chans), pad(upper // 2),
            rows_of(upper), like(F32, 9 * chans, chans), like(F32, 3 * chans, chans), send,
        ],
        copies=9 + levels, after=[token], alias={9: 0},
    )
    piece = (levels, rs + rt, chans)
    if plain:
        parts = (full[: 9 * chans], full[9 * chans : 12 * chans])
        both = jnp.concatenate([g.reshape(levels, 2, dp, -1, chans) for g in parts], axis=3)
        pick = functools.partial(lax.dynamic_index_in_dim, keepdims=False)
        got = lax.ppermute(pick(both, 1 - core[0], 1).astype(BF16), "seq", swap)
        mine = pick(both, core[0], 1) + got.astype(F32)
        own = pick(mine, q[0], 1)
        sends = [pick(mine, peer(q[0], k, dp), 1).astype(BF16) for k in range(1, dp)]
    else:
        got = lax.ppermute(send, "seq", swap)
        own, *sends, token = call(
            functools.partial(split_kernel, dp), "split", "shh v" + "h" * (dp - 1), mac // 8,
            [jnp.concatenate([core, q]), full, got],
            [like(F32, *piece)] + [like(BF16, *piece)] * (dp - 1),
            [like(F32, *send.shape), like(BF16, *send.shape), like(BF16, dp - 1, *piece)],
            copies=2 * levels + dp,
        )
    got = [lax.ppermute(s, "dp", [(i, peer(i, k, dp)) for i in range(dp)]) for k, s in enumerate(sends, 1)]
    cross = lax.ppermute(cross, "seq", down)
    back, token = call(
        functools.partial(back_top_kernel, rows, width), "back_top", "hh h", 9 * mac, [low, sw], [rows_of(height)],
        [rows_of(height // 2 + 2), sw, rows_of(height // 2), wide(height // 2)], copies=3, after=[token],
    )
    level_piece = (rs + rt, chans)
    own, *sends, token = call(
        functools.partial(level_kernel, levels), "level", "sv" + "h" * (dp - 1) + " " + "v" * levels, mac // 8,
        [level, own, *got], [like(F32, *level_piece)] + [like(BF16, *level_piece)] * (levels - 1),
        [like(BF16, dp - 1, *piece)], copies=dp - 1, after=[token],
    )
    got = [
        lax.ppermute(s, "seq", [(i, 2 * peer(i // 2, k, levels) + i % 2) for i in range(seq)])
        for k, s in enumerate(sends, 1)
    ]
    back, token = call(
        functools.partial(back_bottom_kernel, rows, width), "back_bottom", "hhhh h", 9 * mac,
        [low, cross, sw, back], [rows_of(height)],
        [rows_of(height // 2 + 2), rows_of(REMOTE), sw, rows_of(height // 2), wide(height // 2)],
        copies=4, after=[token], alias={3: 0},
    )
    small, token = call(
        sum_kernel, "sum", "v" * levels + " v", mac // 8, [own, *got], [like(BF16, *level_piece)], after=[token]
    )
    got = [lax.ppermute(small, "dp", [(peer(i, k, dp), i) for i in range(dp)]) for k in range(1, dp)]
    spatial, temporal, token = call(
        functools.partial(place_kernel, scale), "place", "s" + "v" * dp + " vv", mac // 8, [q, small, *got],
        [like(F32, dp, rs, chans), like(F32, dp, rt, chans)],
    )
    return (back.reshape(video.shape), spatial.reshape(-1, chans), temporal.reshape(-1, chans))


def solution(mesh):
    placed = (P("dp", "seq", None, None, None), P("dp", "seq", None, None, None), P(), P())
    return jax.shard_map(
        shards,
        mesh=mesh,
        in_specs=placed,
        out_specs=(P("dp", "seq", None, None, None), P("seq", None), P("seq", None)),
        check_vma=False,
    )
```

```python
import functools

import jax
import jax.numpy as jnp
from jax import lax
from jax.experimental import pallas as pl
from jax.experimental.pallas import tpu as pltpu
from jax.sharding import PartitionSpec as P

BF16, F32 = jnp.bfloat16, jnp.float32
EDGE = 8
LIMIT, FULL = 24 * 2**20, 60 * 2**20
REMOTE = 7
SPARE = 45056


def dot(a, b):
    return jnp.dot(a, b, preferred_element_type=F32)


def dot_rt(a, b):
    return lax.dot_general(a, b, (((1,), (1,)), ((), ())), preferred_element_type=F32)


def dot_lt(a, b):
    return lax.dot_general(a, b, (((0,), (0,)), ((), ())), preferred_element_type=F32)


def like(dtype, *shape):
    return jax.ShapeDtypeStruct(shape, dtype)


SPACE = {
    "s": pl.BlockSpec(memory_space=pltpu.SMEM),
    "v": pl.BlockSpec(memory_space=pltpu.VMEM),
    "h": pl.BlockSpec(memory_space=pl.ANY),
}


def call(kernel, name, spaces, flops, args, outs, scratch=(), copies=0, after=(), alias=None, limit=LIMIT):
    nbytes = sum(a.size * a.dtype.itemsize for a in (*args, *outs) if a.shape[0] < SPARE)
    ins, results = spaces.split()
    n_in, n_out = len(args), len(outs)

    def body(*refs):
        rest = refs[n_in + len(after) :]
        kernel(*refs[:n_in], *rest[:n_out], *rest[n_out + 1 :])
        rest[n_out][...] = jnp.zeros(TOKEN.shape, TOKEN.dtype)

    return pl.pallas_call(
        body,
        out_shape=[*outs, TOKEN],
        in_specs=[SPACE[c] for c in ins] + [SPACE["v"]] * len(after),
        out_specs=[SPACE[c] for c in results] + [SPACE["v"]],
        scratch_shapes=[*(pltpu.VMEM(s.shape, s.dtype) for s in scratch), *([pltpu.SemaphoreType.DMA((copies,))] if copies else [])],
        input_output_aliases={} if alias is None else alias,
        compiler_params=pltpu.CompilerParams(vmem_limit_bytes=limit),
        cost_estimate=pl.CostEstimate(flops=flops, bytes_accessed=nbytes, transcendentals=0),
        name=name,
    )(*args, *after)


class Copies:
    def __init__(self, sems):
        self.sems, self.used = sems, 0

    def start(self, *pairs):
        started = []
        for a, b in pairs:
            started.append(pltpu.make_async_copy(a, b, self.sems.at[self.used]))
            self.used += 1
            started[-1].start()
        return started


def wait_all(copies):
    for c in copies:
        c.wait()


def behind(value, token):
    return lax.optimization_barrier((value, token))


TOKEN = like(F32, 8, 128)


def tile(i, size, base=0):
    return pl.ds(pl.multiple_of(base + i * size, size), size)


def loop(steps, body):
    def step(i, carry):
        body(i)
        return carry

    lax.fori_loop(0, steps, step, 0)


def chunk(n):
    return n if n < 8 else max(d for d in range(1, 7) if n % d == 0)


def silu_parts(v):
    v = v.astype(F32)
    sig = 0.5 * jnp.tanh(0.5 * v) + 0.5
    act = v * sig
    return act.astype(BF16), sig + act * (1.0 - sig)


def clear_edges(pad):
    n, long, chans = pad.shape
    pad[:, :EDGE] = jnp.zeros((n, EDGE, chans), F32)
    pad[:, long - EDGE :] = jnp.zeros((n, EDGE, chans), F32)


def put_shifts(cat, where, mid, pad):
    n, long, chans = pad.shape
    width = long - 2 * EDGE
    pad[:, EDGE : EDGE + width] = mid.astype(F32).reshape(n, width, chans)
    cat[where, chans : 2 * chans] = mid
    cat[where, :chans] = pad[:, EDGE + 1 : EDGE + 1 + width].astype(BF16).reshape(n * width, chans)
    cat[where, 2 * chans :] = pad[:, EDGE - 1 : EDGE - 1 + width].astype(BF16).reshape(n * width, chans)


def conv_rows(rows3, tap, out, step, wide):
    width = wide.shape[2] - 2 * EDGE

    def body(i):
        start = i * step
        rows = [rows3[pl.ds(pl.multiple_of(start + a * width, width), step)] for a in range(3)]
        conv_tile(jnp.concatenate(rows, axis=1), tap, out, tile(i, step), wide)

    for side in range(2):
        clear_edges(wide.at[side])
    loop((rows3.shape[0] - 2 * width) // step, body)


def conv_tile(rows, tap, out, where, wide):
    _, n, long, chans = wide.shape
    width = long - 2 * EDGE
    wide[0, :, EDGE : EDGE + width] = tap(rows, 0).reshape(n, width, chans)
    wide[1, :, EDGE : EDGE + width] = tap(rows, 2).reshape(n, width, chans)
    mid = tap(rows, 1).reshape(n, width, chans)
    mid += wide[0, :, EDGE - 1 : EDGE - 1 + width] + wide[1, :, EDGE + 1 : EDGE + 1 + width]
    out[where] = mid.reshape(n * width, chans).astype(BF16)


def forward_tap(sw):
    return lambda rows, b: dot(rows, jnp.concatenate([sw[a, b] for a in range(3)], axis=0))


def back_tap(sw):
    return lambda rows, b: dot_rt(rows, jnp.concatenate([sw[2 - a, 2 - b] for a in range(3)], axis=1))


def tap_parts(video, cat, first, last, base, height, width):
    chans = video.shape[1]
    for a in range(3):
        low, high = max(first, 1 - a), min(last, height + 1 - a)
        rows = video[(low + a - 1 - base) * width : (high + a - 1 - base) * width]
        part = dot_lt(rows, cat[(low - first) * width : (high - first) * width])
        for b in range(3):
            yield 3 * a + b, part[:, b * chans : (b + 1) * chans]


def local_kernel(
    height, width, upper, core, video, cot, mate, sw, tw, act_top, slope_top, rest, cross, spatial, temporal, sw_v, low,
    rows3, both, tw_v, hidden_v, act, cat, wide, pad, grad_v, sems,
):
    rows, chans = video.shape
    top_rows = upper * width
    copies = Copies(sems)
    head = copies.start((video, rows3.at[width : rows + width]), (sw, sw_v))
    tail = copies.start((cot, both.at[:, :chans]), (mate, both.at[:, chans:]), (tw, tw_v))
    rows3[:width] = jnp.zeros((width, chans), BF16)
    rows3[rows + width :] = jnp.zeros((width, chans), BF16)
    clear_edges(pad)
    wait_all(head)
    conv_rows(rows3, forward_tap(sw_v), hidden_v, wide.shape[1] * width, wide)
    wait_all(tail)
    even = core[0] == 0
    tap0 = tw_v[0]
    tap1 = jnp.where(even, tw_v[1], jnp.zeros_like(tap0))
    taps = jnp.concatenate([tap0, tap1], axis=1)
    taps_cross = jnp.concatenate([tw_v[2], jnp.where(even, jnp.zeros_like(tap0), tw_v[1])], axis=1)
    step = pad.shape[0] * width

    def bottom(i):
        here = pl.ds(pl.multiple_of(top_rows + i * step, width), step)
        act_rows, slope = silu_parts(hidden_v[here])
        act[here] = act_rows
        pair = both[here]
        mid = (dot_rt(pair, taps) * slope).astype(BF16)
        cross[tile(i, step)] = dot_rt(pair, taps_cross)
        grad_v[tile(i, step)] = mid
        put_shifts(cat, tile(i, step), mid, pad)

    loop((rows - top_rows) // step, bottom)
    out = copies.start((grad_v, low.at[rows + top_rows : 2 * rows]))
    top_step = chunk(upper) * width

    def top(i):
        here = tile(i, top_step)
        act_rows, slope = silu_parts(hidden_v[here])
        act[here] = act_rows
        act_top[here] = act_rows
        slope_top[here] = slope
        rest[here] = dot_rt(both[here], taps)

    loop(top_rows // top_step, top)
    for tap, part in tap_parts(rows3, cat, upper, height, -1, height, width):
        spatial[tap] = part
    part = dot_lt(act[...], both[...])
    temporal[0] = part[:, :chans]
    temporal[1] = jnp.where(even, part[:, chans:], 0.0)
    temporal[2] = jnp.zeros((chans, chans), F32)
    wait_all(out)


def remote_kernel(
    height, width, upper, core, above, cot, mate, part, sw, spatial, temporal, spatial_out, temporal_out, grad,
    both, other, act, cat, wide, pad, grad_v, sems,
):
    chans = cot.shape[1]
    at = upper * width
    count = part.shape[0]
    copies = Copies(sems)
    tail = copies.start((mate.at[at:], both.at[:, :chans]), (cot.at[at:], both.at[:, chans:]))
    even = core[0] == 0
    clear_edges(pad)
    for side in range(2):
        clear_edges(wide.at[side])
    last = jnp.concatenate([above[2 * width :], jnp.zeros((width, chans), BF16)], axis=0)
    rows = jnp.concatenate([above[:count], above[width : width + count], last], axis=1)
    conv_tile(rows, forward_tap(sw), other, slice(0, count), wide)
    step = pad.shape[0] * width

    def remote(i):
        here = tile(i, step)
        act_rows, slope = silu_parts(other[here])
        act[here] = act_rows
        mid = (part[here] * slope).astype(BF16)
        grad_v[here] = mid
        put_shifts(cat, here, mid, pad)

    loop(count // step, remote)
    out = copies.start((grad_v, grad))
    for tap, part in tap_parts(above, cat, upper, height, upper - 1, height, width):
        spatial_out[tap] = spatial[tap] + part
    wait_all(tail)
    part = dot_lt(act[...], both[...])
    temporal_out[0] = temporal[0]
    temporal_out[1] = temporal[1] + jnp.where(even, 0.0, part[:, :chans])
    temporal_out[2] = temporal[2] + part[:, chans:]
    wait_all(out)


def own_kernel(
    height, width, upper, plain, core, video, act, slope, rest, near, far, tw, spatial, temporal, low_in, low, full, send,
    rows, cat, pad, grad_v, total, total_t, send_v, sems,
):
    count, chans = near.shape
    whole = height * width
    copies = Copies(sems)
    tail = copies.start((video.at[: count + width], rows))
    clear_edges(pad)
    even = core[0] == 0
    taps = jnp.concatenate([jnp.where(even, jnp.zeros_like(tw[1]), tw[1]), tw[2]], axis=1)
    step = pad.shape[0] * width

    def own(i):
        here = tile(i, step)
        grad = rest[here] + dot_rt(jnp.concatenate([near[here], far[here]], axis=1), taps)
        mid = (grad * slope[here]).astype(BF16)
        grad_v[here] = mid
        put_shifts(cat, here, mid, pad)

    loop(count // step, own)
    out = copies.start((grad_v, low.at[whole : whole + count]))
    part = dot_lt(act[...], jnp.concatenate([near[...], far[...]], axis=1))
    total_t[:chans] = temporal[0]
    total_t[chans : 2 * chans] = temporal[1] + jnp.where(even, 0.0, part[:, :chans])
    total_t[2 * chans :] = temporal[2] + part[:, chans:]
    n, first = total.shape[0], 0
    wait_all(tail)
    levels, each = send.shape[:2]
    rt = total_t.shape[0] // (2 * levels)
    rs = each - rt
    for tap, part in tap_parts(rows, cat, 0, upper, 0, height, width):
        total[tap * chans : (tap + 1) * chans] = spatial[tap] + part
        while not plain and first < levels and (first + 1) * 2 * rs <= (tap + 1) * chans:
            theirs, ours = 2 * first + 1 - core[0], 2 * first + core[0]
            send_v[first, :rs] = total[pl.ds(pl.multiple_of(theirs * rs, 8), rs)].astype(BF16)
            send_v[first, rs:] = total_t[pl.ds(pl.multiple_of(theirs * rt, 8), rt)].astype(BF16)
            at = first * each
            out += copies.start(
                (send_v.at[first], send.at[first]),
                (total.at[pl.ds(pl.multiple_of(ours * rs, 8), rs)], full.at[at : at + rs]),
                (total_t.at[pl.ds(pl.multiple_of(ours * rt, 8), rt)], full.at[at + rs : at + each]),
            )
            first += 1
    if plain:
        out += copies.start((total, full.at[:n]), (total_t, full.at[n : n + total_t.shape[0]]))
    wait_all(out)


def back_top_kernel(whole, width, low, sw, back, rows3, sw_v, out, wide, sems):
    chans = out.shape[1]
    held = rows3.shape[0] - width
    copies = Copies(sems)
    head = copies.start((low.at[whole : whole + held], rows3.at[width:]), (sw, sw_v))
    rows3[:width] = jnp.zeros((width, chans), BF16)
    wait_all(head)
    conv_rows(rows3, back_tap(sw_v), out, wide.shape[1] * width, wide)
    wait_all(copies.start((out, back.at[: out.shape[0]])))


def back_bottom_kernel(whole, width, low, got, sw, _, back, rows3, got_v, sw_v, out, wide, sems):
    chans = out.shape[1]
    held = rows3.shape[0] - width
    count = got.shape[0]
    copies = Copies(sems)
    head = copies.start((low.at[2 * whole - held : 2 * whole], rows3.at[:held]), (sw, sw_v))
    head += copies.start((got, got_v))
    rows3[held:] = jnp.zeros((width, chans), BF16)
    wait_all(head)

    def add(i):
        here = pl.ds(pl.multiple_of(held - count + i * width, width), width)
        rows3[here] = (rows3[here].astype(F32) + got_v[tile(i, width)].astype(F32)).astype(BF16)

    loop(count // width, add)
    conv_rows(rows3, back_tap(sw_v), out, wide.shape[1] * width, wide)
    wait_all(copies.start((out, back.at[back.shape[0] - out.shape[0] :])))


def peer(index, k, size):
    return index ^ k if size & (size - 1) == 0 else (index + k) % size


def split_kernel(size, where, kept, swapped, own, *refs):
    sends, (keep_v, sems) = refs[: size - 1], refs[size - 1 :]
    q = where[0]
    levels, each, chans = swapped.shape
    rs = own.shape[1] * 3 // 4
    rt = own.shape[1] - rs
    copies = Copies(sems)
    ins = copies.start(*((kept.at[level * each : (level + 1) * each], keep_v.at[level]) for level in range(levels)))
    for level in range(levels):
        ins[level].wait()
        keep_v[level] += swapped[level].astype(F32)

        def total(i):
            low = keep_v[level, pl.ds(pl.multiple_of(i * rs, 8), rs)]
            return jnp.concatenate([low, keep_v[level, pl.ds(pl.multiple_of(size * rs + i * rt, 8), rt)]], axis=0)

        for k, send in enumerate(sends):
            send[level] = total(peer(q, k + 1, size)).astype(BF16)
        own[level] = total(q)


def level_kernel(size, where, own, *refs):
    got = refs[: -size - 2]
    mine, *sends = refs[-size - 2 : -2]
    got_v, sems = refs[-2:]
    level = where[0]
    copies = Copies(sems)
    wait_all(copies.start(*((g, got_v.at[k]) for k, g in enumerate(got))))

    def total(i):
        return sum((got_v[k, i].astype(F32) for k in range(len(got))), own[i])

    mine[...] = total(level)
    for k, out in enumerate(sends, 1):
        out[...] = total(peer(level, k, size)).astype(BF16)


def sum_kernel(own, *refs):
    *got, out = refs
    out[...] = sum((g[...].astype(F32) for g in got), own[...]).astype(BF16)


def place_kernel(scale, where, small, *refs):
    *got, spatial, temporal = refs
    size, rs, rt = len(got) + 1, spatial.shape[1], temporal.shape[1]
    for k, part in enumerate((small, *got)):
        at = peer(where[0], k, size)
        rows = part[...].astype(F32) * scale
        spatial[at] = rows[:rs]
        temporal[at] = rows[rs:]


def shards(video, cotangent, spatial_weight, temporal_weight):
    height, width, chans = (video.shape[2], video.shape[3], video.shape[4])
    rows = height * width
    dp, seq = lax.axis_size("dp"), lax.axis_size("seq")
    levels = seq // 2
    scale = float((dp * video.shape[0] * seq * rows) ** -0.5)
    dp_at, seq_at = lax.axis_index("dp").astype(jnp.int32), lax.axis_index("seq").astype(jnp.int32)
    core, level, q = (v.reshape(1) for v in (seq_at % 2, seq_at // 2, dp_at))
    x = video.reshape(rows, chans)
    cot = cotangent.reshape(rows, chans)
    sw, tw = spatial_weight, temporal_weight
    upper = height - REMOTE
    down = [(i + 2, i) for i in range(seq - 2)]
    up = [(i, i + 2) for i in range(seq - 2)]
    swap = [(i, i ^ 1) for i in range(seq)]

    mac = rows * chans * chans
    long = width + 2 * EDGE
    taps9, taps3 = (like(F32, n, chans, chans) for n in (9, 3))

    def rows_of(n, columns=chans, dtype=BF16):
        return like(dtype, n * width, columns)

    def wide(n):
        return like(F32, 2, n, long, chans)

    mate = lax.ppermute(cot, "seq", swap)
    far = lax.ppermute(cot[: upper * width], "seq", down)
    above = lax.ppermute(x[(upper - 1) * width :], "seq", up)

    def pad(n):
        return like(F32, n, long, chans)

    act, slope, rest, part, spatial, temporal, sw_v, low, token = call(
        functools.partial(local_kernel, height, width, upper), "local", "shhhhh vvvvvvvh", 34 * mac, [core, x, cot, mate, sw, tw],
        [
            rows_of(upper), rows_of(upper, dtype=F32), rows_of(upper, dtype=F32), rows_of(REMOTE, dtype=F32), taps9, taps3, sw,
            like(BF16, 2 * SPARE, chans),
        ],
        [
            rows_of(height + 2), rows_of(height, 2 * chans), tw, rows_of(height), rows_of(height),
            rows_of(REMOTE, 3 * chans), wide(height // 2), pad(chunk(REMOTE)), rows_of(REMOTE),
        ],
        copies=6,
    )
    far, token = behind(far, token)
    near = lax.ppermute(far, "seq", swap)
    spatial, temporal, cross, token = call(
        functools.partial(remote_kernel, height, width, upper), "remote", "svhhvvvv vvh", 16 * mac,
        [core, above, cot, mate, part, sw_v, spatial, temporal], [taps9, taps3, rows_of(REMOTE)],
        [
            rows_of(REMOTE, 2 * chans), rows_of(REMOTE), rows_of(REMOTE),
            rows_of(REMOTE, 3 * chans), wide(REMOTE), pad(chunk(REMOTE)), rows_of(REMOTE),
        ],
        copies=3, after=[token],
    )
    rs, rt = 9 * chans // (seq * dp), 3 * chans // (seq * dp)
    plain = bool(rs % 8 or rt % 8 or dp * rs % 16 or dp * rt % 16)
    send = like(BF16, levels, dp * (rs + rt), chans)
    low, full, send, token = call(
        functools.partial(own_kernel, height, width, upper, plain), "own", "shvvvvvvvvh hhh", 16 * mac,
        [core, x, act, slope, rest, near, far, tw, spatial, temporal, low], [low, like(F32, SPARE, chans), send],
        [
            rows_of(upper + 1), rows_of(upper, 3 * chans), pad(chunk(upper)),
            rows_of(upper), like(F32, 9 * chans, chans), like(F32, 3 * chans, chans), send,
        ],
        copies=4 + 3 * levels, after=[token], alias={10: 0},
    )
    piece = (levels, rs + rt, chans)
    if plain:
        parts = (full[: 9 * chans], full[9 * chans : 12 * chans])
        both = jnp.concatenate([g.reshape(levels, 2, dp, -1, chans) for g in parts], axis=3)
        pick = functools.partial(lax.dynamic_index_in_dim, keepdims=False)
        got = lax.ppermute(pick(both, 1 - core[0], 1).astype(BF16), "seq", swap)
        mine = pick(both, core[0], 1) + got.astype(F32)
        own = pick(mine, q[0], 1)
        sends = [pick(mine, peer(q[0], k, dp), 1).astype(BF16) for k in range(1, dp)]
    else:
        got = lax.ppermute(send, "seq", swap)
        own, *sends, token = call(
            functools.partial(split_kernel, dp), "split", "shv v" + "v" * (dp - 1), mac // 8,
            [q, full, got],
            [like(F32, *piece)] + [like(BF16, *piece)] * (dp - 1),
            [like(F32, *send.shape)], copies=levels,
        )
    got = [lax.ppermute(s, "dp", [(i, peer(i, k, dp)) for i in range(dp)]) for k, s in enumerate(sends, 1)]
    cross = lax.ppermute(cross, "seq", down)
    back, token = call(
        functools.partial(back_top_kernel, rows, width), "back_top", "hh h", 9 * mac, [low, sw], [rows_of(height)],
        [rows_of(height // 2 + 2), sw, rows_of(height // 2), wide(height // 2)], copies=3, after=[token],
    )
    level_piece = (rs + rt, chans)
    own, *sends, token = call(
        functools.partial(level_kernel, levels), "level", "sv" + "h" * (dp - 1) + " " + "v" * levels, mac // 8,
        [level, own, *got], [like(F32, *level_piece)] + [like(BF16, *level_piece)] * (levels - 1),
        [like(BF16, dp - 1, *piece)], copies=dp - 1, after=[token],
    )
    got = [
        lax.ppermute(s, "seq", [(i, 2 * peer(i // 2, k, levels) + i % 2) for i in range(seq)])
        for k, s in enumerate(sends, 1)
    ]
    back, token = call(
        functools.partial(back_bottom_kernel, rows, width), "back_bottom", "hhhh h", 9 * mac,
        [low, cross, sw, back], [rows_of(height)],
        [rows_of(height // 2 + 2), rows_of(REMOTE), sw, rows_of(height // 2), wide(height // 2)],
        copies=4, after=[token], alias={3: 0},
    )
    small, token = call(
        sum_kernel, "sum", "v" * levels + " v", mac // 8, [own, *got], [like(BF16, *level_piece)], after=[token]
    )
    got = [lax.ppermute(small, "dp", [(peer(i, k, dp), i) for i in range(dp)]) for k in range(1, dp)]
    spatial, temporal, token = call(
        functools.partial(place_kernel, scale), "place", "s" + "v" * dp + " vv", mac // 8, [q, small, *got],
        [like(F32, dp, rs, chans), like(F32, dp, rt, chans)],
    )
    return (back.reshape(video.shape), spatial.reshape(-1, chans), temporal.reshape(-1, chans))


def solution(mesh):
    placed = (P("dp", "seq", None, None, None), P("dp", "seq", None, None, None), P(), P())
    return jax.shard_map(
        shards,
        mesh=mesh,
        in_specs=placed,
        out_specs=(P("dp", "seq", None, None, None), P("seq", None), P("seq", None)),
        check_vma=False,
    )
```

```python
import functools

import jax
import jax.numpy as jnp
from jax import lax
from jax.experimental import pallas as pl
from jax.experimental.pallas import tpu as pltpu
from jax.sharding import PartitionSpec as P

BF16, F32 = jnp.bfloat16, jnp.float32
EDGE = 8
LIMIT, FULL = 24 * 2**20, 60 * 2**20
REMOTE = 7
SPARE = 45056


def dot(a, b):
    return jnp.dot(a, b, preferred_element_type=F32)


def dot_rt(a, b):
    return lax.dot_general(a, b, (((1,), (1,)), ((), ())), preferred_element_type=F32)


def dot_lt(a, b):
    return lax.dot_general(a, b, (((0,), (0,)), ((), ())), preferred_element_type=F32)


def like(dtype, *shape):
    return jax.ShapeDtypeStruct(shape, dtype)


SPACE = {
    "s": pl.BlockSpec(memory_space=pltpu.SMEM),
    "v": pl.BlockSpec(memory_space=pltpu.VMEM),
    "h": pl.BlockSpec(memory_space=pl.ANY),
}


def call(kernel, name, spaces, flops, args, outs, scratch=(), copies=0, after=(), alias=None, limit=LIMIT):
    nbytes = sum(a.size * a.dtype.itemsize for a in (*args, *outs) if a.shape[0] < SPARE)
    ins, results = spaces.split()
    n_in, n_out = len(args), len(outs)

    def body(*refs):
        rest = refs[n_in + len(after) :]
        kernel(*refs[:n_in], *rest[:n_out], *rest[n_out + 1 :])
        rest[n_out][...] = jnp.zeros(TOKEN.shape, TOKEN.dtype)

    return pl.pallas_call(
        body,
        out_shape=[*outs, TOKEN],
        in_specs=[SPACE[c] for c in ins] + [SPACE["v"]] * len(after),
        out_specs=[SPACE[c] for c in results] + [SPACE["v"]],
        scratch_shapes=[*(pltpu.VMEM(s.shape, s.dtype) for s in scratch), *([pltpu.SemaphoreType.DMA((copies,))] if copies else [])],
        input_output_aliases={} if alias is None else alias,
        compiler_params=pltpu.CompilerParams(vmem_limit_bytes=limit),
        cost_estimate=pl.CostEstimate(flops=flops, bytes_accessed=nbytes, transcendentals=0),
        name=name,
    )(*args, *after)


class Copies:
    def __init__(self, sems):
        self.sems, self.used = sems, 0

    def start(self, *pairs):
        started = []
        for a, b in pairs:
            started.append(pltpu.make_async_copy(a, b, self.sems.at[self.used]))
            self.used += 1
            started[-1].start()
        return started


def wait_all(copies):
    for c in copies:
        c.wait()


def behind(value, token):
    return lax.optimization_barrier((value, token))


TOKEN = like(F32, 8, 128)


def tile(i, size, base=0):
    return pl.ds(pl.multiple_of(base + i * size, size), size)


def loop(steps, body):
    def step(i, carry):
        body(i)
        return carry

    lax.fori_loop(0, steps, step, 0)


def chunk(n):
    return n if n < 8 else max(d for d in range(1, 7) if n % d == 0)


def silu_parts(v):
    v = v.astype(F32)
    sig = 0.5 * jnp.tanh(0.5 * v) + 0.5
    act = v * sig
    return act.astype(BF16), sig + act * (1.0 - sig)


def clear_edges(pad):
    n, long, chans = pad.shape
    pad[:, :EDGE] = jnp.zeros((n, EDGE, chans), F32)
    pad[:, long - EDGE :] = jnp.zeros((n, EDGE, chans), F32)


def put_shifts(cat, where, mid, pad):
    n, long, chans = pad.shape
    width = long - 2 * EDGE
    pad[:, EDGE : EDGE + width] = mid.astype(F32).reshape(n, width, chans)
    cat[where, chans : 2 * chans] = mid
    cat[where, :chans] = pad[:, EDGE + 1 : EDGE + 1 + width].astype(BF16).reshape(n * width, chans)
    cat[where, 2 * chans :] = pad[:, EDGE - 1 : EDGE - 1 + width].astype(BF16).reshape(n * width, chans)


def conv_rows(rows3, tap, out, step, wide):
    width = wide.shape[2] - 2 * EDGE

    def body(i):
        start = i * step
        rows = [rows3[pl.ds(pl.multiple_of(start + a * width, width), step)] for a in range(3)]
        conv_tile(jnp.concatenate(rows, axis=1), tap, out, tile(i, step), wide)

    for side in range(2):
        clear_edges(wide.at[side])
    loop((rows3.shape[0] - 2 * width) // step, body)


def conv_tile(rows, tap, out, where, wide):
    _, n, long, chans = wide.shape
    width = long - 2 * EDGE
    wide[0, :, EDGE : EDGE + width] = tap(rows, 0).reshape(n, width, chans)
    wide[1, :, EDGE : EDGE + width] = tap(rows, 2).reshape(n, width, chans)
    mid = tap(rows, 1).reshape(n, width, chans)
    mid += wide[0, :, EDGE - 1 : EDGE - 1 + width] + wide[1, :, EDGE + 1 : EDGE + 1 + width]
    out[where] = mid.reshape(n * width, chans).astype(BF16)


def forward_tap(sw):
    return lambda rows, b: dot(rows, jnp.concatenate([sw[a, b] for a in range(3)], axis=0))


def back_tap(sw):
    return lambda rows, b: dot_rt(rows, jnp.concatenate([sw[2 - a, 2 - b] for a in range(3)], axis=1))


def tap_parts(video, cat, first, last, base, height, width):
    chans = video.shape[1]
    for a in range(3):
        low, high = max(first, 1 - a), min(last, height + 1 - a)
        rows = video[(low + a - 1 - base) * width : (high + a - 1 - base) * width]
        part = dot_lt(rows, cat[(low - first) * width : (high - first) * width])
        for b in range(3):
            yield 3 * a + b, part[:, b * chans : (b + 1) * chans]


def local_kernel(
    height, width, upper, core, video, cot, mate, sw, tw, act_top, slope_top, rest, cross, spatial, temporal, sw_v, low,
    rows3, both, tw_v, hidden_v, act, cat, wide, pad, grad_v, sems,
):
    rows, chans = video.shape
    top_rows = upper * width
    copies = Copies(sems)
    head = copies.start((video, rows3.at[width : rows + width]), (sw, sw_v))
    tail = copies.start((cot, both.at[:, :chans]), (mate, both.at[:, chans:]), (tw, tw_v))
    rows3[:width] = jnp.zeros((width, chans), BF16)
    rows3[rows + width :] = jnp.zeros((width, chans), BF16)
    clear_edges(pad)
    wait_all(head)
    conv_rows(rows3, forward_tap(sw_v), hidden_v, wide.shape[1] * width, wide)
    wait_all(tail)
    even = core[0] == 0
    tap0 = tw_v[0]
    tap1 = jnp.where(even, tw_v[1], jnp.zeros_like(tap0))
    taps = jnp.concatenate([tap0, tap1], axis=1)
    taps_cross = jnp.concatenate([tw_v[2], jnp.where(even, jnp.zeros_like(tap0), tw_v[1])], axis=1)
    step = pad.shape[0] * width

    def bottom(i):
        here = pl.ds(pl.multiple_of(top_rows + i * step, width), step)
        act_rows, slope = silu_parts(hidden_v[here])
        act[here] = act_rows
        pair = both[here]
        mid = (dot_rt(pair, taps) * slope).astype(BF16)
        cross[tile(i, step)] = dot_rt(pair, taps_cross)
        grad_v[tile(i, step)] = mid
        put_shifts(cat, tile(i, step), mid, pad)

    loop((rows - top_rows) // step, bottom)
    out = copies.start((grad_v, low.at[rows + top_rows : 2 * rows]))
    top_step = chunk(upper) * width

    def top(i):
        here = tile(i, top_step)
        act_rows, slope = silu_parts(hidden_v[here])
        act[here] = act_rows
        act_top[here] = act_rows
        slope_top[here] = slope
        rest[here] = dot_rt(both[here], taps)

    loop(top_rows // top_step, top)
    for tap, part in tap_parts(rows3, cat, upper, height, -1, height, width):
        spatial[tap] = part
    part = dot_lt(act[...], both[...])
    temporal[0] = part[:, :chans]
    temporal[1] = jnp.where(even, part[:, chans:], 0.0)
    temporal[2] = jnp.zeros((chans, chans), F32)
    wait_all(out)


def remote_kernel(
    height, width, upper, core, above, cot, mate, part, sw, spatial, temporal, spatial_out, temporal_out, grad,
    both, other, act, cat, wide, pad, grad_v, sems,
):
    chans = cot.shape[1]
    at = upper * width
    count = part.shape[0]
    copies = Copies(sems)
    tail = copies.start((mate.at[at:], both.at[:, :chans]), (cot.at[at:], both.at[:, chans:]))
    even = core[0] == 0
    clear_edges(pad)
    for side in range(2):
        clear_edges(wide.at[side])
    last = jnp.concatenate([above[2 * width :], jnp.zeros((width, chans), BF16)], axis=0)
    rows = jnp.concatenate([above[:count], above[width : width + count], last], axis=1)
    conv_tile(rows, forward_tap(sw), other, slice(0, count), wide)
    step = pad.shape[0] * width

    def remote(i):
        here = tile(i, step)
        act_rows, slope = silu_parts(other[here])
        act[here] = act_rows
        mid = (part[here] * slope).astype(BF16)
        grad_v[here] = mid
        put_shifts(cat, here, mid, pad)

    loop(count // step, remote)
    out = copies.start((grad_v, grad))
    for tap, part in tap_parts(above, cat, upper, height, upper - 1, height, width):
        spatial_out[tap] = spatial[tap] + part
    wait_all(tail)
    part = dot_lt(act[...], both[...])
    temporal_out[0] = temporal[0]
    temporal_out[1] = temporal[1] + jnp.where(even, 0.0, part[:, :chans])
    temporal_out[2] = temporal[2] + part[:, chans:]
    wait_all(out)


def own_kernel(
    height, width, upper, plain, core, video, act, slope, rest, near, far, tw, spatial, temporal, low_in, low, full, send,
    rows, cat, pad, grad_v, total, total_t, send_v, sems,
):
    count, chans = near.shape
    whole = height * width
    copies = Copies(sems)
    tail = copies.start((video.at[: count + width], rows))
    clear_edges(pad)
    even = core[0] == 0
    taps = jnp.concatenate([jnp.where(even, jnp.zeros_like(tw[1]), tw[1]), tw[2]], axis=1)
    step = pad.shape[0] * width

    def own(i):
        here = tile(i, step)
        grad = rest[here] + dot_rt(jnp.concatenate([near[here], far[here]], axis=1), taps)
        mid = (grad * slope[here]).astype(BF16)
        grad_v[here] = mid
        put_shifts(cat, here, mid, pad)

    loop(count // step, own)
    out = copies.start((grad_v, low.at[whole : whole + count]))
    part = dot_lt(act[...], jnp.concatenate([near[...], far[...]], axis=1))
    total_t[:chans] = temporal[0]
    total_t[chans : 2 * chans] = temporal[1] + jnp.where(even, 0.0, part[:, :chans])
    total_t[2 * chans :] = temporal[2] + part[:, chans:]
    n, first = total.shape[0], 0
    wait_all(tail)
    levels, each = send.shape[:2]
    rt = total_t.shape[0] // (2 * levels)
    rs = each - rt
    for tap, part in tap_parts(rows, cat, 0, upper, 0, height, width):
        total[tap * chans : (tap + 1) * chans] = spatial[tap] + part
        while not plain and first < levels and (first + 1) * 2 * rs <= (tap + 1) * chans:
            theirs, ours = 2 * first + 1 - core[0], 2 * first + core[0]
            send_v[first, :rs] = total[pl.ds(pl.multiple_of(theirs * rs, 8), rs)].astype(BF16)
            send_v[first, rs:] = total_t[pl.ds(pl.multiple_of(theirs * rt, 8), rt)].astype(BF16)
            at = first * each
            out += copies.start(
                (send_v.at[first], send.at[first]),
                (total.at[pl.ds(pl.multiple_of(ours * rs, 8), rs)], full.at[at : at + rs]),
                (total_t.at[pl.ds(pl.multiple_of(ours * rt, 8), rt)], full.at[at + rs : at + each]),
            )
            first += 1
    if plain:
        out += copies.start((total, full.at[:n]), (total_t, full.at[n : n + total_t.shape[0]]))
    wait_all(out)


def back_top_kernel(whole, width, low, sw, back, rows3, sw_v, out, wide, sems):
    chans = out.shape[1]
    held = rows3.shape[0] - width
    copies = Copies(sems)
    head = copies.start((low.at[whole : whole + held], rows3.at[width:]), (sw, sw_v))
    rows3[:width] = jnp.zeros((width, chans), BF16)
    wait_all(head)
    conv_rows(rows3, back_tap(sw_v), out, wide.shape[1] * width, wide)
    wait_all(copies.start((out, back.at[: out.shape[0]])))


def back_bottom_kernel(whole, width, low, got, sw, _, back, rows3, got_v, sw_v, out, wide, sems):
    chans = out.shape[1]
    held = rows3.shape[0] - width
    count = got.shape[0]
    copies = Copies(sems)
    head = copies.start((low.at[2 * whole - held : 2 * whole], rows3.at[:held]), (sw, sw_v))
    head += copies.start((got, got_v))
    rows3[held:] = jnp.zeros((width, chans), BF16)
    wait_all(head)

    def add(i):
        here = pl.ds(pl.multiple_of(held - count + i * width, width), width)
        rows3[here] = (rows3[here].astype(F32) + got_v[tile(i, width)].astype(F32)).astype(BF16)

    loop(count // width, add)
    conv_rows(rows3, back_tap(sw_v), out, wide.shape[1] * width, wide)
    wait_all(copies.start((out, back.at[back.shape[0] - out.shape[0] :])))


def peer(index, k, size):
    return index ^ k if size & (size - 1) == 0 else (index + k) % size


def split_kernel(size, where, kept, swapped, own, *refs):
    sends, (keep_v, sems) = refs[: size - 1], refs[size - 1 :]
    q = where[0]
    levels, each, chans = swapped.shape
    rs = own.shape[1] * 3 // 4
    rt = own.shape[1] - rs
    copies = Copies(sems)
    ins = copies.start(*((kept.at[level * each : (level + 1) * each], keep_v.at[level]) for level in range(levels)))
    for level in range(levels):
        ins[level].wait()
        keep_v[level] += swapped[level].astype(F32)

        def total(i):
            low = keep_v[level, pl.ds(pl.multiple_of(i * rs, 8), rs)]
            return jnp.concatenate([low, keep_v[level, pl.ds(pl.multiple_of(size * rs + i * rt, 8), rt)]], axis=0)

        for k, send in enumerate(sends):
            send[level] = total(peer(q, k + 1, size)).astype(BF16)
        own[level] = total(q)


def level_kernel(size, where, own, *refs):
    got = refs[: -size - 2]
    mine, *sends = refs[-size - 2 : -2]
    got_v, sems = refs[-2:]
    level = where[0]
    copies = Copies(sems)
    wait_all(copies.start(*((g, got_v.at[k]) for k, g in enumerate(got))))

    def total(i):
        return sum((got_v[k, i].astype(F32) for k in range(len(got))), own[i])

    mine[...] = total(level)
    for k, out in enumerate(sends, 1):
        out[...] = total(peer(level, k, size)).astype(BF16)


def sum_kernel(own, *refs):
    *got, out = refs
    out[...] = sum((g[...].astype(F32) for g in got), own[...]).astype(BF16)


def place_kernel(scale, where, small, *refs):
    *got, spatial, temporal = refs
    size, rs, rt = len(got) + 1, spatial.shape[1], temporal.shape[1]
    for k, part in enumerate((small, *got)):
        at = peer(where[0], k, size)
        rows = part[...].astype(F32) * scale
        spatial[at] = rows[:rs]
        temporal[at] = rows[rs:]


def shards(video, cotangent, spatial_weight, temporal_weight):
    height, width, chans = (video.shape[2], video.shape[3], video.shape[4])
    rows = height * width
    dp, seq = lax.axis_size("dp"), lax.axis_size("seq")
    levels = seq // 2
    scale = float((dp * video.shape[0] * seq * rows) ** -0.5)
    dp_at, seq_at = lax.axis_index("dp").astype(jnp.int32), lax.axis_index("seq").astype(jnp.int32)
    core, level, q = (v.reshape(1) for v in (seq_at % 2, seq_at // 2, dp_at))
    x = video.reshape(rows, chans)
    cot = cotangent.reshape(rows, chans)
    sw, tw = spatial_weight, temporal_weight
    upper = height - REMOTE
    down = [(i + 2, i) for i in range(seq - 2)]
    up = [(i, i + 2) for i in range(seq - 2)]
    swap = [(i, i ^ 1) for i in range(seq)]

    mac = rows * chans * chans
    long = width + 2 * EDGE
    taps9, taps3 = (like(F32, n, chans, chans) for n in (9, 3))

    def rows_of(n, columns=chans, dtype=BF16):
        return like(dtype, n * width, columns)

    def wide(n):
        return like(F32, 2, n, long, chans)

    mate = lax.ppermute(cot, "seq", swap)
    far = lax.ppermute(cot[: upper * width], "seq", down)
    above, mate = lax.optimization_barrier((x[(upper - 1) * width :], mate))
    above = lax.ppermute(above, "seq", up)

    def pad(n):
        return like(F32, n, long, chans)

    act, slope, rest, part, spatial, temporal, sw_v, low, token = call(
        functools.partial(local_kernel, height, width, upper), "local", "shhhhh vvvvvvvh", 34 * mac, [core, x, cot, mate, sw, tw],
        [
            rows_of(upper), rows_of(upper, dtype=F32), rows_of(upper, dtype=F32), rows_of(REMOTE, dtype=F32), taps9, taps3, sw,
            like(BF16, 2 * SPARE, chans),
        ],
        [
            rows_of(height + 2), rows_of(height, 2 * chans), tw, rows_of(height), rows_of(height),
            rows_of(REMOTE, 3 * chans), wide(height // 2), pad(chunk(REMOTE)), rows_of(REMOTE),
        ],
        copies=6,
    )
    far, token = behind(far, token)
    near = lax.ppermute(far, "seq", swap)
    spatial, temporal, cross, token = call(
        functools.partial(remote_kernel, height, width, upper), "remote", "svhhvvvv vvh", 16 * mac,
        [core, above, cot, mate, part, sw_v, spatial, temporal], [taps9, taps3, rows_of(REMOTE)],
        [
            rows_of(REMOTE, 2 * chans), rows_of(REMOTE), rows_of(REMOTE),
            rows_of(REMOTE, 3 * chans), wide(REMOTE), pad(chunk(REMOTE)), rows_of(REMOTE),
        ],
        copies=3, after=[token],
    )
    rs, rt = 9 * chans // (seq * dp), 3 * chans // (seq * dp)
    plain = bool(rs % 8 or rt % 8 or dp * rs % 16 or dp * rt % 16)
    send = like(BF16, levels, dp * (rs + rt), chans)
    low, full, send, token = call(
        functools.partial(own_kernel, height, width, upper, plain), "own", "shvvvvvvvvh hhh", 16 * mac,
        [core, x, act, slope, rest, near, far, tw, spatial, temporal, low], [low, like(F32, SPARE, chans), send],
        [
            rows_of(upper + 1), rows_of(upper, 3 * chans), pad(chunk(upper)),
            rows_of(upper), like(F32, 9 * chans, chans), like(F32, 3 * chans, chans), send,
        ],
        copies=4 + 3 * levels, after=[token], alias={10: 0},
    )
    piece = (levels, rs + rt, chans)
    if plain:
        parts = (full[: 9 * chans], full[9 * chans : 12 * chans])
        both = jnp.concatenate([g.reshape(levels, 2, dp, -1, chans) for g in parts], axis=3)
        pick = functools.partial(lax.dynamic_index_in_dim, keepdims=False)
        got = lax.ppermute(pick(both, 1 - core[0], 1).astype(BF16), "seq", swap)
        mine = pick(both, core[0], 1) + got.astype(F32)
        own = pick(mine, q[0], 1)
        sends = [pick(mine, peer(q[0], k, dp), 1).astype(BF16) for k in range(1, dp)]
    else:
        got = lax.ppermute(send, "seq", swap)
        own, *sends, token = call(
            functools.partial(split_kernel, dp), "split", "shv v" + "v" * (dp - 1), mac // 8,
            [q, full, got],
            [like(F32, *piece)] + [like(BF16, *piece)] * (dp - 1),
            [like(F32, *send.shape)], copies=levels,
        )
    got = [lax.ppermute(s, "dp", [(i, peer(i, k, dp)) for i in range(dp)]) for k, s in enumerate(sends, 1)]
    cross = lax.ppermute(cross, "seq", down)
    back, token = call(
        functools.partial(back_top_kernel, rows, width), "back_top", "hh h", 9 * mac, [low, sw], [rows_of(height)],
        [rows_of(height // 2 + 2), sw, rows_of(height // 2), wide(height // 2)], copies=3, after=[token],
    )
    level_piece = (rs + rt, chans)
    own, *sends, token = call(
        functools.partial(level_kernel, levels), "level", "sv" + "h" * (dp - 1) + " " + "v" * levels, mac // 8,
        [level, own, *got], [like(F32, *level_piece)] + [like(BF16, *level_piece)] * (levels - 1),
        [like(BF16, dp - 1, *piece)], copies=dp - 1, after=[token],
    )
    got = [
        lax.ppermute(s, "seq", [(i, 2 * peer(i // 2, k, levels) + i % 2) for i in range(seq)])
        for k, s in enumerate(sends, 1)
    ]
    back, token = call(
        functools.partial(back_bottom_kernel, rows, width), "back_bottom", "hhhh h", 9 * mac,
        [low, cross, sw, back], [rows_of(height)],
        [rows_of(height // 2 + 2), rows_of(REMOTE), sw, rows_of(height // 2), wide(height // 2)],
        copies=4, after=[token], alias={3: 0},
    )
    small, token = call(
        sum_kernel, "sum", "v" * levels + " v", mac // 8, [own, *got], [like(BF16, *level_piece)], after=[token]
    )
    got = [lax.ppermute(small, "dp", [(peer(i, k, dp), i) for i in range(dp)]) for k in range(1, dp)]
    spatial, temporal, token = call(
        functools.partial(place_kernel, scale), "place", "s" + "v" * dp + " vv", mac // 8, [q, small, *got],
        [like(F32, dp, rs, chans), like(F32, dp, rt, chans)],
    )
    return (back.reshape(video.shape), spatial.reshape(-1, chans), temporal.reshape(-1, chans))


def solution(mesh):
    placed = (P("dp", "seq", None, None, None), P("dp", "seq", None, None, None), P(), P())
    return jax.shard_map(
        shards,
        mesh=mesh,
        in_specs=placed,
        out_specs=(P("dp", "seq", None, None, None), P("seq", None), P("seq", None)),
        check_vma=False,
    )
```

```python
import functools

import jax
import jax.numpy as jnp
from jax import lax
from jax.experimental import pallas as pl
from jax.experimental.pallas import tpu as pltpu
from jax.sharding import PartitionSpec as P

BF16, F32 = jnp.bfloat16, jnp.float32
EDGE = 8
LIMIT, FULL = 24 * 2**20, 60 * 2**20
REMOTE = 7
SPARE = 45056


def dot(a, b):
    return jnp.dot(a, b, preferred_element_type=F32)


def dot_rt(a, b):
    return lax.dot_general(a, b, (((1,), (1,)), ((), ())), preferred_element_type=F32)


def dot_lt(a, b):
    return lax.dot_general(a, b, (((0,), (0,)), ((), ())), preferred_element_type=F32)


def like(dtype, *shape):
    return jax.ShapeDtypeStruct(shape, dtype)


SPACE = {
    "s": pl.BlockSpec(memory_space=pltpu.SMEM),
    "v": pl.BlockSpec(memory_space=pltpu.VMEM),
    "h": pl.BlockSpec(memory_space=pl.ANY),
}


def call(kernel, name, spaces, flops, args, outs, scratch=(), copies=0, after=(), alias=None, limit=LIMIT):
    nbytes = sum(a.size * a.dtype.itemsize for a in (*args, *outs) if a.shape[0] < SPARE)
    ins, results = spaces.split()
    n_in, n_out = len(args), len(outs)

    def body(*refs):
        rest = refs[n_in + len(after) :]
        kernel(*refs[:n_in], *rest[:n_out], *rest[n_out + 1 :])
        rest[n_out][...] = jnp.zeros(TOKEN.shape, TOKEN.dtype)

    return pl.pallas_call(
        body,
        out_shape=[*outs, TOKEN],
        in_specs=[SPACE[c] for c in ins] + [SPACE["v"]] * len(after),
        out_specs=[SPACE[c] for c in results] + [SPACE["v"]],
        scratch_shapes=[*(pltpu.VMEM(s.shape, s.dtype) for s in scratch), *([pltpu.SemaphoreType.DMA((copies,))] if copies else [])],
        input_output_aliases={} if alias is None else alias,
        compiler_params=pltpu.CompilerParams(vmem_limit_bytes=limit),
        cost_estimate=pl.CostEstimate(flops=flops, bytes_accessed=nbytes, transcendentals=0),
        name=name,
    )(*args, *after)


class Copies:
    def __init__(self, sems):
        self.sems, self.used = sems, 0

    def start(self, *pairs):
        started = []
        for a, b in pairs:
            started.append(pltpu.make_async_copy(a, b, self.sems.at[self.used]))
            self.used += 1
            started[-1].start()
        return started


def wait_all(copies):
    for c in copies:
        c.wait()


def behind(value, token):
    return lax.optimization_barrier((value, token))


TOKEN = like(F32, 8, 128)


def tile(i, size, base=0):
    return pl.ds(pl.multiple_of(base + i * size, size), size)


def loop(steps, body):
    def step(i, carry):
        body(i)
        return carry

    lax.fori_loop(0, steps, step, 0)


def chunk(n):
    return n if n < 10 else max(d for d in range(1, 7) if n % d == 0)


def silu_parts(v):
    v = v.astype(F32)
    sig = 0.5 * jnp.tanh(0.5 * v) + 0.5
    act = v * sig
    return act.astype(BF16), sig + act * (1.0 - sig)


def clear_edges(pad):
    n, long, chans = pad.shape
    pad[:, :EDGE] = jnp.zeros((n, EDGE, chans), F32)
    pad[:, long - EDGE :] = jnp.zeros((n, EDGE, chans), F32)


def put_shifts(cat, where, mid, pad):
    n, long, chans = pad.shape
    width = long - 2 * EDGE
    pad[:, EDGE : EDGE + width] = mid.astype(F32).reshape(n, width, chans)
    cat[where, chans : 2 * chans] = mid
    cat[where, :chans] = pad[:, EDGE + 1 : EDGE + 1 + width].astype(BF16).reshape(n * width, chans)
    cat[where, 2 * chans :] = pad[:, EDGE - 1 : EDGE - 1 + width].astype(BF16).reshape(n * width, chans)


def conv_rows(rows3, tap, out, step, wide):
    width = wide.shape[2] - 2 * EDGE

    def body(i):
        start = i * step
        rows = [rows3[pl.ds(pl.multiple_of(start + a * width, width), step)] for a in range(3)]
        conv_tile(jnp.concatenate(rows, axis=1), tap, out, tile(i, step), wide)

    for side in range(2):
        clear_edges(wide.at[side])
    loop((rows3.shape[0] - 2 * width) // step, body)


def conv_tile(rows, tap, out, where, wide):
    _, n, long, chans = wide.shape
    width = long - 2 * EDGE
    wide[0, :, EDGE : EDGE + width] = tap(rows, 0).reshape(n, width, chans)
    wide[1, :, EDGE : EDGE + width] = tap(rows, 2).reshape(n, width, chans)
    mid = tap(rows, 1).reshape(n, width, chans)
    mid += wide[0, :, EDGE - 1 : EDGE - 1 + width] + wide[1, :, EDGE + 1 : EDGE + 1 + width]
    out[where] = mid.reshape(n * width, chans).astype(BF16)


def forward_tap(sw):
    return lambda rows, b: dot(rows, jnp.concatenate([sw[a, b] for a in range(3)], axis=0))


def back_tap(sw):
    return lambda rows, b: dot_rt(rows, jnp.concatenate([sw[2 - a, 2 - b] for a in range(3)], axis=1))


def tap_parts(video, cat, first, last, base, height, width):
    chans = video.shape[1]
    for a in range(3):
        low, high = max(first, 1 - a), min(last, height + 1 - a)
        rows = video[(low + a - 1 - base) * width : (high + a - 1 - base) * width]
        part = dot_lt(rows, cat[(low - first) * width : (high - first) * width])
        for b in range(3):
            yield 3 * a + b, part[:, b * chans : (b + 1) * chans]


def local_kernel(
    height, width, upper, core, video, cot, mate, sw, tw, act_top, slope_top, rest, cross, spatial, temporal, sw_v, low,
    rows3, both, tw_v, hidden_v, act, cat, wide, pad, grad_v, sems,
):
    rows, chans = video.shape
    top_rows = upper * width
    copies = Copies(sems)
    head = copies.start((video, rows3.at[width : rows + width]), (sw, sw_v))
    tail = copies.start((cot, both.at[:, :chans]), (mate, both.at[:, chans:]), (tw, tw_v))
    rows3[:width] = jnp.zeros((width, chans), BF16)
    rows3[rows + width :] = jnp.zeros((width, chans), BF16)
    clear_edges(pad)
    wait_all(head)
    conv_rows(rows3, forward_tap(sw_v), hidden_v, wide.shape[1] * width, wide)
    wait_all(tail)
    even = core[0] == 0
    tap0 = tw_v[0]
    tap1 = jnp.where(even, tw_v[1], jnp.zeros_like(tap0))
    taps = jnp.concatenate([tap0, tap1], axis=1)
    taps_cross = jnp.concatenate([tw_v[2], jnp.where(even, jnp.zeros_like(tap0), tw_v[1])], axis=1)
    step = pad.shape[0] * width

    def bottom(i):
        here = pl.ds(pl.multiple_of(top_rows + i * step, width), step)
        act_rows, slope = silu_parts(hidden_v[here])
        act[here] = act_rows
        pair = both[here]
        mid = (dot_rt(pair, taps) * slope).astype(BF16)
        cross[tile(i, step)] = dot_rt(pair, taps_cross)
        grad_v[tile(i, step)] = mid
        put_shifts(cat, tile(i, step), mid, pad)

    loop((rows - top_rows) // step, bottom)
    out = copies.start((grad_v, low.at[rows + top_rows : 2 * rows]))
    top_step = chunk(upper) * width

    def top(i):
        here = tile(i, top_step)
        act_rows, slope = silu_parts(hidden_v[here])
        act[here] = act_rows
        act_top[here] = act_rows
        slope_top[here] = slope
        rest[here] = dot_rt(both[here], taps)

    loop(top_rows // top_step, top)
    for tap, part in tap_parts(rows3, cat, upper, height, -1, height, width):
        spatial[tap] = part
    part = dot_lt(act[...], both[...])
    temporal[0] = part[:, :chans]
    temporal[1] = jnp.where(even, part[:, chans:], 0.0)
    temporal[2] = jnp.zeros((chans, chans), F32)
    wait_all(out)


def remote_kernel(
    height, width, upper, core, above, cot, mate, part, sw, spatial, temporal, spatial_out, temporal_out, grad,
    both, other, act, cat, wide, pad, grad_v, sems,
):
    chans = cot.shape[1]
    at = upper * width
    count = part.shape[0]
    copies = Copies(sems)
    tail = copies.start((mate.at[at:], both.at[:, :chans]), (cot.at[at:], both.at[:, chans:]))
    even = core[0] == 0
    clear_edges(pad)
    for side in range(2):
        clear_edges(wide.at[side])
    last = jnp.concatenate([above[2 * width :], jnp.zeros((width, chans), BF16)], axis=0)
    rows = jnp.concatenate([above[:count], above[width : width + count], last], axis=1)
    conv_tile(rows, forward_tap(sw), other, slice(0, count), wide)
    step = pad.shape[0] * width

    def remote(i):
        here = tile(i, step)
        act_rows, slope = silu_parts(other[here])
        act[here] = act_rows
        mid = (part[here] * slope).astype(BF16)
        grad_v[here] = mid
        put_shifts(cat, here, mid, pad)

    loop(count // step, remote)
    out = copies.start((grad_v, grad))
    for tap, part in tap_parts(above, cat, upper, height, upper - 1, height, width):
        spatial_out[tap] = spatial[tap] + part
    wait_all(tail)
    part = dot_lt(act[...], both[...])
    temporal_out[0] = temporal[0]
    temporal_out[1] = temporal[1] + jnp.where(even, 0.0, part[:, :chans])
    temporal_out[2] = temporal[2] + part[:, chans:]
    wait_all(out)


def own_kernel(
    height, width, upper, plain, core, video, act, slope, rest, near, far, tw, spatial, temporal, low_in, low, full, send,
    rows, cat, pad, grad_v, total, total_t, send_v, sems,
):
    count, chans = near.shape
    whole = height * width
    copies = Copies(sems)
    tail = copies.start((video.at[: count + width], rows))
    clear_edges(pad)
    even = core[0] == 0
    taps = jnp.concatenate([jnp.where(even, jnp.zeros_like(tw[1]), tw[1]), tw[2]], axis=1)
    step = pad.shape[0] * width

    def own(i):
        here = tile(i, step)
        grad = rest[here] + dot_rt(jnp.concatenate([near[here], far[here]], axis=1), taps)
        mid = (grad * slope[here]).astype(BF16)
        grad_v[here] = mid
        put_shifts(cat, here, mid, pad)

    loop(count // step, own)
    out = copies.start((grad_v, low.at[whole : whole + count]))
    part = dot_lt(act[...], jnp.concatenate([near[...], far[...]], axis=1))
    total_t[:chans] = temporal[0]
    total_t[chans : 2 * chans] = temporal[1] + jnp.where(even, 0.0, part[:, :chans])
    total_t[2 * chans :] = temporal[2] + part[:, chans:]
    n, first = total.shape[0], 0
    wait_all(tail)
    levels, each = send.shape[:2]
    rt = total_t.shape[0] // (2 * levels)
    rs = each - rt
    for tap, part in tap_parts(rows, cat, 0, upper, 0, height, width):
        total[tap * chans : (tap + 1) * chans] = spatial[tap] + part
        while not plain and first < levels and (first + 1) * 2 * rs <= (tap + 1) * chans:
            theirs, ours = 2 * first + 1 - core[0], 2 * first + core[0]
            send_v[first, :rs] = total[pl.ds(pl.multiple_of(theirs * rs, 8), rs)].astype(BF16)
            send_v[first, rs:] = total_t[pl.ds(pl.multiple_of(theirs * rt, 8), rt)].astype(BF16)
            at = first * each
            out += copies.start(
                (send_v.at[first], send.at[first]),
                (total.at[pl.ds(pl.multiple_of(ours * rs, 8), rs)], full.at[at : at + rs]),
                (total_t.at[pl.ds(pl.multiple_of(ours * rt, 8), rt)], full.at[at + rs : at + each]),
            )
            first += 1
    if plain:
        out += copies.start((total, full.at[:n]), (total_t, full.at[n : n + total_t.shape[0]]))
    wait_all(out)


def back_top_kernel(whole, width, low, sw, back, rows3, sw_v, out, wide, sems):
    chans = out.shape[1]
    held = rows3.shape[0] - width
    copies = Copies(sems)
    head = copies.start((low.at[whole : whole + held], rows3.at[width:]), (sw, sw_v))
    rows3[:width] = jnp.zeros((width, chans), BF16)
    wait_all(head)
    conv_rows(rows3, back_tap(sw_v), out, wide.shape[1] * width, wide)
    wait_all(copies.start((out, back.at[: out.shape[0]])))


def back_bottom_kernel(whole, width, low, got, sw, _, back, rows3, got_v, sw_v, out, wide, sems):
    chans = out.shape[1]
    held = rows3.shape[0] - width
    count = got.shape[0]
    copies = Copies(sems)
    head = copies.start((low.at[2 * whole - held : 2 * whole], rows3.at[:held]), (sw, sw_v))
    head += copies.start((got, got_v))
    rows3[held:] = jnp.zeros((width, chans), BF16)
    wait_all(head)

    def add(i):
        here = pl.ds(pl.multiple_of(held - count + i * width, width), width)
        rows3[here] = (rows3[here].astype(F32) + got_v[tile(i, width)].astype(F32)).astype(BF16)

    loop(count // width, add)
    conv_rows(rows3, back_tap(sw_v), out, wide.shape[1] * width, wide)
    wait_all(copies.start((out, back.at[back.shape[0] - out.shape[0] :])))


def peer(index, k, size):
    return index ^ k if size & (size - 1) == 0 else (index + k) % size


def split_kernel(size, where, kept, swapped, own, *refs):
    sends, (keep_v, sems) = refs[: size - 1], refs[size - 1 :]
    q = where[0]
    levels, each, chans = swapped.shape
    rs = own.shape[1] * 3 // 4
    rt = own.shape[1] - rs
    copies = Copies(sems)
    ins = copies.start(*((kept.at[level * each : (level + 1) * each], keep_v.at[level]) for level in range(levels)))
    for level in range(levels):
        ins[level].wait()
        keep_v[level] += swapped[level].astype(F32)

        def total(i):
            low = keep_v[level, pl.ds(pl.multiple_of(i * rs, 8), rs)]
            return jnp.concatenate([low, keep_v[level, pl.ds(pl.multiple_of(size * rs + i * rt, 8), rt)]], axis=0)

        for k, send in enumerate(sends):
            send[level] = total(peer(q, k + 1, size)).astype(BF16)
        own[level] = total(q)


def level_kernel(size, where, own, *refs):
    got = refs[: -size - 2]
    mine, *sends = refs[-size - 2 : -2]
    got_v, sems = refs[-2:]
    level = where[0]
    copies = Copies(sems)
    wait_all(copies.start(*((g, got_v.at[k]) for k, g in enumerate(got))))

    def total(i):
        return sum((got_v[k, i].astype(F32) for k in range(len(got))), own[i])

    mine[...] = total(level)
    for k, out in enumerate(sends, 1):
        out[...] = total(peer(level, k, size)).astype(BF16)


def sum_kernel(own, *refs):
    *got, out = refs
    out[...] = sum((g[...].astype(F32) for g in got), own[...]).astype(BF16)


def place_kernel(scale, where, small, *refs):
    *got, spatial, temporal = refs
    size, rs, rt = len(got) + 1, spatial.shape[1], temporal.shape[1]
    for k, part in enumerate((small, *got)):
        at = peer(where[0], k, size)
        rows = part[...].astype(F32) * scale
        spatial[at] = rows[:rs]
        temporal[at] = rows[rs:]


def shards(video, cotangent, spatial_weight, temporal_weight):
    height, width, chans = (video.shape[2], video.shape[3], video.shape[4])
    rows = height * width
    dp, seq = lax.axis_size("dp"), lax.axis_size("seq")
    levels = seq // 2
    scale = float((dp * video.shape[0] * seq * rows) ** -0.5)
    dp_at, seq_at = lax.axis_index("dp").astype(jnp.int32), lax.axis_index("seq").astype(jnp.int32)
    core, level, q = (v.reshape(1) for v in (seq_at % 2, seq_at // 2, dp_at))
    x = video.reshape(rows, chans)
    cot = cotangent.reshape(rows, chans)
    sw, tw = spatial_weight, temporal_weight
    upper = height - REMOTE
    down = [(i + 2, i) for i in range(seq - 2)]
    up = [(i, i + 2) for i in range(seq - 2)]
    swap = [(i, i ^ 1) for i in range(seq)]

    mac = rows * chans * chans
    long = width + 2 * EDGE
    taps9, taps3 = (like(F32, n, chans, chans) for n in (9, 3))

    def rows_of(n, columns=chans, dtype=BF16):
        return like(dtype, n * width, columns)

    def wide(n):
        return like(F32, 2, n, long, chans)

    mate = lax.ppermute(cot, "seq", swap)
    far = lax.ppermute(cot[: upper * width], "seq", down)
    above, mate = lax.optimization_barrier((x[(upper - 1) * width :], mate))
    above = lax.ppermute(above, "seq", up)

    def pad(n):
        return like(F32, n, long, chans)

    act, slope, rest, part, spatial, temporal, sw_v, low, token = call(
        functools.partial(local_kernel, height, width, upper), "local", "shhhhh vvvvvvvh", 34 * mac, [core, x, cot, mate, sw, tw],
        [
            rows_of(upper), rows_of(upper, dtype=F32), rows_of(upper, dtype=F32), rows_of(REMOTE, dtype=F32), taps9, taps3, sw,
            like(BF16, 2 * SPARE, chans),
        ],
        [
            rows_of(height + 2), rows_of(height, 2 * chans), tw, rows_of(height), rows_of(height),
            rows_of(REMOTE, 3 * chans), wide(height // 2), pad(chunk(REMOTE)), rows_of(REMOTE),
        ],
        copies=6,
    )
    far, token = behind(far, token)
    near = lax.ppermute(far, "seq", swap)
    spatial, temporal, cross, token = call(
        functools.partial(remote_kernel, height, width, upper), "remote", "svhhvvvv vvh", 16 * mac,
        [core, above, cot, mate, part, sw_v, spatial, temporal], [taps9, taps3, rows_of(REMOTE)],
        [
            rows_of(REMOTE, 2 * chans), rows_of(REMOTE), rows_of(REMOTE),
            rows_of(REMOTE, 3 * chans), wide(REMOTE), pad(chunk(REMOTE)), rows_of(REMOTE),
        ],
        copies=3, after=[token],
    )
    rs, rt = 9 * chans // (seq * dp), 3 * chans // (seq * dp)
    plain = bool(rs % 8 or rt % 8 or dp * rs % 16 or dp * rt % 16)
    send = like(BF16, levels, dp * (rs + rt), chans)
    low, full, send, token = call(
        functools.partial(own_kernel, height, width, upper, plain), "own", "shvvvvvvvvh hhh", 16 * mac,
        [core, x, act, slope, rest, near, far, tw, spatial, temporal, low], [low, like(F32, SPARE, chans), send],
        [
            rows_of(upper + 1), rows_of(upper, 3 * chans), pad(chunk(upper)),
            rows_of(upper), like(F32, 9 * chans, chans), like(F32, 3 * chans, chans), send,
        ],
        copies=4 + 3 * levels, after=[token], alias={10: 0},
    )
    piece = (levels, rs + rt, chans)
    if plain:
        parts = (full[: 9 * chans], full[9 * chans : 12 * chans])
        both = jnp.concatenate([g.reshape(levels, 2, dp, -1, chans) for g in parts], axis=3)
        pick = functools.partial(lax.dynamic_index_in_dim, keepdims=False)
        got = lax.ppermute(pick(both, 1 - core[0], 1).astype(BF16), "seq", swap)
        mine = pick(both, core[0], 1) + got.astype(F32)
        own = pick(mine, q[0], 1)
        sends = [pick(mine, peer(q[0], k, dp), 1).astype(BF16) for k in range(1, dp)]
    else:
        got = lax.ppermute(send, "seq", swap)
        own, *sends, token = call(
            functools.partial(split_kernel, dp), "split", "shv v" + "v" * (dp - 1), mac // 8,
            [q, full, got],
            [like(F32, *piece)] + [like(BF16, *piece)] * (dp - 1),
            [like(F32, *send.shape)], copies=levels,
        )
    got = [lax.ppermute(s, "dp", [(i, peer(i, k, dp)) for i in range(dp)]) for k, s in enumerate(sends, 1)]
    cross = lax.ppermute(cross, "seq", down)
    back, token = call(
        functools.partial(back_top_kernel, rows, width), "back_top", "hh h", 9 * mac, [low, sw], [rows_of(height)],
        [rows_of(height // 2 + 2), sw, rows_of(height // 2), wide(height // 2)], copies=3, after=[token],
    )
    level_piece = (rs + rt, chans)
    own, *sends, token = call(
        functools.partial(level_kernel, levels), "level", "sv" + "h" * (dp - 1) + " " + "v" * levels, mac // 8,
        [level, own, *got], [like(F32, *level_piece)] + [like(BF16, *level_piece)] * (levels - 1),
        [like(BF16, dp - 1, *piece)], copies=dp - 1, after=[token],
    )
    got = [
        lax.ppermute(s, "seq", [(i, 2 * peer(i // 2, k, levels) + i % 2) for i in range(seq)])
        for k, s in reversed(list(enumerate(sends, 1)))
    ]
    back, token = call(
        functools.partial(back_bottom_kernel, rows, width), "back_bottom", "hhhh h", 9 * mac,
        [low, cross, sw, back], [rows_of(height)],
        [rows_of(height // 2 + 2), rows_of(REMOTE), sw, rows_of(height // 2), wide(height // 2)],
        copies=4, after=[token], alias={3: 0},
    )
    small, token = call(
        sum_kernel, "sum", "v" * levels + " v", mac // 8, [own, *got], [like(BF16, *level_piece)], after=[token]
    )
    got = [lax.ppermute(small, "dp", [(peer(i, k, dp), i) for i in range(dp)]) for k in range(1, dp)]
    spatial, temporal, token = call(
        functools.partial(place_kernel, scale), "place", "s" + "v" * dp + " vv", mac // 8, [q, small, *got],
        [like(F32, dp, rs, chans), like(F32, dp, rt, chans)],
    )
    return (back.reshape(video.shape), spatial.reshape(-1, chans), temporal.reshape(-1, chans))


def solution(mesh):
    placed = (P("dp", "seq", None, None, None), P("dp", "seq", None, None, None), P(), P())
    return jax.shard_map(
        shards,
        mesh=mesh,
        in_specs=placed,
        out_specs=(P("dp", "seq", None, None, None), P("seq", None), P("seq", None)),
        check_vma=False,
    )
```

```python
import functools

import jax
import jax.numpy as jnp
from jax import lax
from jax.experimental import pallas as pl
from jax.experimental.pallas import tpu as pltpu
from jax.sharding import PartitionSpec as P

BF16, F32 = jnp.bfloat16, jnp.float32
EDGE = 8
LIMIT, FULL = 24 * 2**20, 60 * 2**20
REMOTE = 7
SPARE = 45056


def dot(a, b):
    return jnp.dot(a, b, preferred_element_type=F32)


def dot_rt(a, b):
    return lax.dot_general(a, b, (((1,), (1,)), ((), ())), preferred_element_type=F32)


def dot_lt(a, b):
    return lax.dot_general(a, b, (((0,), (0,)), ((), ())), preferred_element_type=F32)


def like(dtype, *shape):
    return jax.ShapeDtypeStruct(shape, dtype)


SPACE = {
    "s": pl.BlockSpec(memory_space=pltpu.SMEM),
    "v": pl.BlockSpec(memory_space=pltpu.VMEM),
    "h": pl.BlockSpec(memory_space=pl.ANY),
}


def call(kernel, name, spaces, flops, args, outs, scratch=(), copies=0, after=(), alias=None, limit=LIMIT):
    nbytes = sum(a.size * a.dtype.itemsize for a in (*args, *outs) if a.shape[0] < SPARE)
    ins, results = spaces.split()
    n_in, n_out = len(args), len(outs)

    def body(*refs):
        rest = refs[n_in + len(after) :]
        kernel(*refs[:n_in], *rest[:n_out], *rest[n_out + 1 :])

    return pl.pallas_call(
        body,
        out_shape=[*outs, TOKEN],
        in_specs=[SPACE[c] for c in ins] + [SPACE["h"]] * len(after),
        out_specs=[SPACE[c] for c in results] + [SPACE["h"]],
        scratch_shapes=[*(pltpu.VMEM(s.shape, s.dtype) for s in scratch), *([pltpu.SemaphoreType.DMA((copies,))] if copies else [])],
        input_output_aliases={} if alias is None else alias,
        compiler_params=pltpu.CompilerParams(vmem_limit_bytes=limit),
        cost_estimate=pl.CostEstimate(flops=flops, bytes_accessed=nbytes, transcendentals=0),
        name=name,
    )(*args, *after)


class Copies:
    def __init__(self, sems):
        self.sems, self.used = sems, 0

    def start(self, *pairs):
        started = []
        for a, b in pairs:
            started.append(pltpu.make_async_copy(a, b, self.sems.at[self.used]))
            self.used += 1
            started[-1].start()
        return started


def wait_all(copies):
    for c in copies:
        c.wait()


def behind(value, token):
    return lax.optimization_barrier((value, token))


TOKEN = like(F32, 8, 128)


def tile(i, size, base=0):
    return pl.ds(pl.multiple_of(base + i * size, size), size)


def loop(steps, body):
    def step(i, carry):
        body(i)
        return carry

    lax.fori_loop(0, steps, step, 0)


def chunk(n):
    return n if n < 10 else max(d for d in range(1, 7) if n % d == 0)


def silu_parts(v):
    v = v.astype(F32)
    sig = 0.5 * jnp.tanh(0.5 * v) + 0.5
    act = v * sig
    return act.astype(BF16), sig + act * (1.0 - sig)


def clear_edges(pad):
    n, long, chans = pad.shape
    pad[:, :EDGE] = jnp.zeros((n, EDGE, chans), F32)
    pad[:, long - EDGE :] = jnp.zeros((n, EDGE, chans), F32)


def put_shifts(cat, where, mid, pad):
    n, long, chans = pad.shape
    width = long - 2 * EDGE
    pad[:, EDGE : EDGE + width] = mid.astype(F32).reshape(n, width, chans)
    cat[where, chans : 2 * chans] = mid
    cat[where, :chans] = pad[:, EDGE + 1 : EDGE + 1 + width].astype(BF16).reshape(n * width, chans)
    cat[where, 2 * chans :] = pad[:, EDGE - 1 : EDGE - 1 + width].astype(BF16).reshape(n * width, chans)


def conv_rows(rows3, tap, out, step, wide):
    width = wide.shape[2] - 2 * EDGE

    def body(i):
        start = i * step
        rows = [rows3[pl.ds(pl.multiple_of(start + a * width, width), step)] for a in range(3)]
        conv_tile(jnp.concatenate(rows, axis=1), tap, out, tile(i, step), wide)

    for side in range(2):
        clear_edges(wide.at[side])
    loop((rows3.shape[0] - 2 * width) // step, body)


def conv_tile(rows, tap, out, where, wide):
    _, n, long, chans = wide.shape
    width = long - 2 * EDGE
    wide[0, :, EDGE : EDGE + width] = tap(rows, 0).reshape(n, width, chans)
    wide[1, :, EDGE : EDGE + width] = tap(rows, 2).reshape(n, width, chans)
    mid = tap(rows, 1).reshape(n, width, chans)
    mid += wide[0, :, EDGE - 1 : EDGE - 1 + width] + wide[1, :, EDGE + 1 : EDGE + 1 + width]
    out[where] = mid.reshape(n * width, chans).astype(BF16)


def forward_tap(sw):
    return lambda rows, b: dot(rows, jnp.concatenate([sw[a, b] for a in range(3)], axis=0))


def back_tap(sw):
    return lambda rows, b: dot_rt(rows, jnp.concatenate([sw[2 - a, 2 - b] for a in range(3)], axis=1))


def tap_parts(video, cat, first, last, base, height, width):
    chans = video.shape[1]
    for a in range(3):
        low, high = max(first, 1 - a), min(last, height + 1 - a)
        rows = video[(low + a - 1 - base) * width : (high + a - 1 - base) * width]
        part = dot_lt(rows, cat[(low - first) * width : (high - first) * width])
        for b in range(3):
            yield 3 * a + b, part[:, b * chans : (b + 1) * chans]


def local_kernel(
    height, width, upper, core, video, cot, mate, sw, tw, act_top, slope_top, rest, cross, spatial, temporal, sw_v, low,
    rows3, both, tw_v, hidden_v, act, cat, wide, pad, grad_v, sems,
):
    rows, chans = video.shape
    top_rows = upper * width
    copies = Copies(sems)
    head = copies.start((video, rows3.at[width : rows + width]), (sw, sw_v))
    tail = copies.start((cot, both.at[:, :chans]), (mate, both.at[:, chans:]), (tw, tw_v))
    rows3[:width] = jnp.zeros((width, chans), BF16)
    rows3[rows + width :] = jnp.zeros((width, chans), BF16)
    clear_edges(pad)
    wait_all(head)
    conv_rows(rows3, forward_tap(sw_v), hidden_v, wide.shape[1] * width, wide)
    wait_all(tail)
    even = core[0] == 0
    tap0 = tw_v[0]
    tap1 = jnp.where(even, tw_v[1], jnp.zeros_like(tap0))
    taps = jnp.concatenate([tap0, tap1], axis=1)
    taps_cross = jnp.concatenate([tw_v[2], jnp.where(even, jnp.zeros_like(tap0), tw_v[1])], axis=1)
    step = pad.shape[0] * width

    def bottom(i):
        here = pl.ds(pl.multiple_of(top_rows + i * step, width), step)
        act_rows, slope = silu_parts(hidden_v[here])
        act[here] = act_rows
        pair = both[here]
        mid = (dot_rt(pair, taps) * slope).astype(BF16)
        cross[tile(i, step)] = dot_rt(pair, taps_cross)
        grad_v[tile(i, step)] = mid
        put_shifts(cat, tile(i, step), mid, pad)

    loop((rows - top_rows) // step, bottom)
    out = copies.start((grad_v, low.at[rows + top_rows : 2 * rows]))
    top_step = chunk(upper) * width

    def top(i):
        here = tile(i, top_step)
        act_rows, slope = silu_parts(hidden_v[here])
        act[here] = act_rows
        act_top[here] = act_rows
        slope_top[here] = slope
        rest[here] = dot_rt(both[here], taps)

    loop(top_rows // top_step, top)
    for tap, part in tap_parts(rows3, cat, upper, height, -1, height, width):
        spatial[tap] = part
    part = dot_lt(act[...], both[...])
    temporal[0] = part[:, :chans]
    temporal[1] = jnp.where(even, part[:, chans:], 0.0)
    temporal[2] = jnp.zeros((chans, chans), F32)
    wait_all(out)


def remote_kernel(
    height, width, upper, core, above, cot, mate, part, sw, spatial, temporal, spatial_out, temporal_out, grad,
    both, other, act, cat, wide, pad, grad_v, sems,
):
    chans = cot.shape[1]
    at = upper * width
    count = part.shape[0]
    copies = Copies(sems)
    tail = copies.start((mate.at[at:], both.at[:, :chans]), (cot.at[at:], both.at[:, chans:]))
    even = core[0] == 0
    clear_edges(pad)
    for side in range(2):
        clear_edges(wide.at[side])
    last = jnp.concatenate([above[2 * width :], jnp.zeros((width, chans), BF16)], axis=0)
    rows = jnp.concatenate([above[:count], above[width : width + count], last], axis=1)
    conv_tile(rows, forward_tap(sw), other, slice(0, count), wide)
    step = pad.shape[0] * width

    def remote(i):
        here = tile(i, step)
        act_rows, slope = silu_parts(other[here])
        act[here] = act_rows
        mid = (part[here] * slope).astype(BF16)
        grad_v[here] = mid
        put_shifts(cat, here, mid, pad)

    loop(count // step, remote)
    out = copies.start((grad_v, grad))
    for tap, part in tap_parts(above, cat, upper, height, upper - 1, height, width):
        spatial_out[tap] = spatial[tap] + part
    wait_all(tail)
    part = dot_lt(act[...], both[...])
    temporal_out[0] = temporal[0]
    temporal_out[1] = temporal[1] + jnp.where(even, 0.0, part[:, :chans])
    temporal_out[2] = temporal[2] + part[:, chans:]
    wait_all(out)


def own_kernel(
    height, width, upper, plain, core, video, act, slope, rest, near, far, tw, spatial, temporal, low_in, low, full, send,
    rows, cat, pad, grad_v, total, total_t, send_v, sems,
):
    count, chans = near.shape
    whole = height * width
    copies = Copies(sems)
    tail = copies.start((video.at[: count + width], rows))
    clear_edges(pad)
    even = core[0] == 0
    taps = jnp.concatenate([jnp.where(even, jnp.zeros_like(tw[1]), tw[1]), tw[2]], axis=1)
    step = pad.shape[0] * width

    def own(i):
        here = tile(i, step)
        grad = rest[here] + dot_rt(jnp.concatenate([near[here], far[here]], axis=1), taps)
        mid = (grad * slope[here]).astype(BF16)
        grad_v[here] = mid
        put_shifts(cat, here, mid, pad)

    loop(count // step, own)
    out = copies.start((grad_v, low.at[whole : whole + count]))
    part = dot_lt(act[...], jnp.concatenate([near[...], far[...]], axis=1))
    total_t[:chans] = temporal[0]
    total_t[chans : 2 * chans] = temporal[1] + jnp.where(even, 0.0, part[:, :chans])
    total_t[2 * chans :] = temporal[2] + part[:, chans:]
    n, first = total.shape[0], 0
    wait_all(tail)
    levels, each = send.shape[:2]
    rt = total_t.shape[0] // (2 * levels)
    rs = each - rt
    for tap, part in tap_parts(rows, cat, 0, upper, 0, height, width):
        total[tap * chans : (tap + 1) * chans] = spatial[tap] + part
        while not plain and first < levels and (first + 1) * 2 * rs <= (tap + 1) * chans:
            theirs, ours = 2 * first + 1 - core[0], 2 * first + core[0]
            send_v[first, :rs] = total[pl.ds(pl.multiple_of(theirs * rs, 8), rs)].astype(BF16)
            send_v[first, rs:] = total_t[pl.ds(pl.multiple_of(theirs * rt, 8), rt)].astype(BF16)
            at = first * each
            out += copies.start(
                (send_v.at[first], send.at[first]),
                (total.at[pl.ds(pl.multiple_of(ours * rs, 8), rs)], full.at[at : at + rs]),
                (total_t.at[pl.ds(pl.multiple_of(ours * rt, 8), rt)], full.at[at + rs : at + each]),
            )
            first += 1
    if plain:
        out += copies.start((total, full.at[:n]), (total_t, full.at[n : n + total_t.shape[0]]))
    wait_all(out)


def back_top_kernel(whole, width, low, sw, back, rows3, sw_v, out, wide, sems):
    chans = out.shape[1]
    held = rows3.shape[0] - width
    copies = Copies(sems)
    head = copies.start((low.at[whole : whole + held], rows3.at[width:]), (sw, sw_v))
    rows3[:width] = jnp.zeros((width, chans), BF16)
    wait_all(head)
    conv_rows(rows3, back_tap(sw_v), out, wide.shape[1] * width, wide)
    wait_all(copies.start((out, back.at[: out.shape[0]])))


def back_bottom_kernel(whole, width, low, got, sw, _, back, rows3, got_v, sw_v, out, wide, sems):
    chans = out.shape[1]
    held = rows3.shape[0] - width
    count = got.shape[0]
    copies = Copies(sems)
    head = copies.start((low.at[2 * whole - held : 2 * whole], rows3.at[:held]), (sw, sw_v))
    head += copies.start((got, got_v))
    rows3[held:] = jnp.zeros((width, chans), BF16)
    wait_all(head)

    def add(i):
        here = pl.ds(pl.multiple_of(held - count + i * width, width), width)
        rows3[here] = (rows3[here].astype(F32) + got_v[tile(i, width)].astype(F32)).astype(BF16)

    loop(count // width, add)
    conv_rows(rows3, back_tap(sw_v), out, wide.shape[1] * width, wide)
    wait_all(copies.start((out, back.at[back.shape[0] - out.shape[0] :])))


def peer(index, k, size):
    return index ^ k if size & (size - 1) == 0 else (index + k) % size


def split_kernel(size, where, kept, swapped, own, *refs):
    sends, (keep_v, sems) = refs[: size - 1], refs[size - 1 :]
    q = where[0]
    levels, each, chans = swapped.shape
    rs = own.shape[1] * 3 // 4
    rt = own.shape[1] - rs
    copies = Copies(sems)
    ins = copies.start(*((kept.at[level * each : (level + 1) * each], keep_v.at[level]) for level in range(levels)))
    for level in range(levels):
        ins[level].wait()
        keep_v[level] += swapped[level].astype(F32)

        def total(i):
            low = keep_v[level, pl.ds(pl.multiple_of(i * rs, 8), rs)]
            return jnp.concatenate([low, keep_v[level, pl.ds(pl.multiple_of(size * rs + i * rt, 8), rt)]], axis=0)

        for k, send in enumerate(sends):
            send[level] = total(peer(q, k + 1, size)).astype(BF16)
        own[level] = total(q)


def level_kernel(size, where, own, *refs):
    got = refs[:-size]
    mine, *sends = refs[-size:]
    level = where[0]

    def total(i):
        return sum((g[i].astype(F32) for g in got), own[i])

    mine[...] = total(level)
    for k, out in enumerate(sends, 1):
        out[...] = total(peer(level, k, size)).astype(BF16)


def sum_kernel(own, *refs):
    *got, out = refs
    out[...] = sum((g[...].astype(F32) for g in got), own[...]).astype(BF16)


def place_kernel(scale, where, small, *refs):
    *got, spatial, temporal = refs
    size, rs, rt = len(got) + 1, spatial.shape[1], temporal.shape[1]
    for k, part in enumerate((small, *got)):
        at = peer(where[0], k, size)
        rows = part[...].astype(F32) * scale
        spatial[at] = rows[:rs]
        temporal[at] = rows[rs:]


def shards(video, cotangent, spatial_weight, temporal_weight):
    height, width, chans = (video.shape[2], video.shape[3], video.shape[4])
    rows = height * width
    dp, seq = lax.axis_size("dp"), lax.axis_size("seq")
    levels = seq // 2
    scale = float((dp * video.shape[0] * seq * rows) ** -0.5)
    dp_at, seq_at = lax.axis_index("dp").astype(jnp.int32), lax.axis_index("seq").astype(jnp.int32)
    core, level, q = (v.reshape(1) for v in (seq_at % 2, seq_at // 2, dp_at))
    x = video.reshape(rows, chans)
    cot = cotangent.reshape(rows, chans)
    sw, tw = spatial_weight, temporal_weight
    upper = height - REMOTE
    down = [(i + 2, i) for i in range(seq - 2)]
    up = [(i, i + 2) for i in range(seq - 2)]
    swap = [(i, i ^ 1) for i in range(seq)]

    mac = rows * chans * chans
    long = width + 2 * EDGE
    taps9, taps3 = (like(F32, n, chans, chans) for n in (9, 3))

    def rows_of(n, columns=chans, dtype=BF16):
        return like(dtype, n * width, columns)

    def wide(n):
        return like(F32, 2, n, long, chans)

    mate = lax.ppermute(cot, "seq", swap)
    far = lax.ppermute(cot[: upper * width], "seq", down)
    above, mate = lax.optimization_barrier((x[(upper - 1) * width :], mate))
    above = lax.ppermute(above, "seq", up)

    def pad(n):
        return like(F32, n, long, chans)

    act, slope, rest, part, spatial, temporal, sw_v, low, token = call(
        functools.partial(local_kernel, height, width, upper), "local", "shhhhh vvvvvvvh", 34 * mac, [core, x, cot, mate, sw, tw],
        [
            rows_of(upper), rows_of(upper, dtype=F32), rows_of(upper, dtype=F32), rows_of(REMOTE, dtype=F32), taps9, taps3, sw,
            like(BF16, 2 * SPARE, chans),
        ],
        [
            rows_of(height + 2), rows_of(height, 2 * chans), tw, rows_of(height), rows_of(height),
            rows_of(REMOTE, 3 * chans), wide(height // 2), pad(chunk(REMOTE)), rows_of(REMOTE),
        ],
        copies=6,
    )
    far, token = behind(far, token)
    near = lax.ppermute(far, "seq", swap)
    spatial, temporal, cross, token = call(
        functools.partial(remote_kernel, height, width, upper), "remote", "svhhvvvv vvh", 16 * mac,
        [core, above, cot, mate, part, sw_v, spatial, temporal], [taps9, taps3, rows_of(REMOTE)],
        [
            rows_of(REMOTE, 2 * chans), rows_of(REMOTE), rows_of(REMOTE),
            rows_of(REMOTE, 3 * chans), wide(REMOTE), pad(chunk(REMOTE)), rows_of(REMOTE),
        ],
        copies=3, after=[token],
    )
    rs, rt = 9 * chans // (seq * dp), 3 * chans // (seq * dp)
    plain = bool(rs % 8 or rt % 8 or dp * rs % 16 or dp * rt % 16)
    send = like(BF16, levels, dp * (rs + rt), chans)
    low, full, send, token = call(
        functools.partial(own_kernel, height, width, upper, plain), "own", "shvvvvvvvvh hhh", 16 * mac,
        [core, x, act, slope, rest, near, far, tw, spatial, temporal, low], [low, like(F32, SPARE, chans), send],
        [
            rows_of(upper + 1), rows_of(upper, 3 * chans), pad(chunk(upper)),
            rows_of(upper), like(F32, 9 * chans, chans), like(F32, 3 * chans, chans), send,
        ],
        copies=4 + 3 * levels, after=[token], alias={10: 0},
    )
    piece = (levels, rs + rt, chans)
    if plain:
        parts = (full[: 9 * chans], full[9 * chans : 12 * chans])
        both = jnp.concatenate([g.reshape(levels, 2, dp, -1, chans) for g in parts], axis=3)
        pick = functools.partial(lax.dynamic_index_in_dim, keepdims=False)
        got = lax.ppermute(pick(both, 1 - core[0], 1).astype(BF16), "seq", swap)
        mine = pick(both, core[0], 1) + got.astype(F32)
        own = pick(mine, q[0], 1)
        sends = [pick(mine, peer(q[0], k, dp), 1).astype(BF16) for k in range(1, dp)]
    else:
        got = lax.ppermute(send, "seq", swap)
        own, *sends, token = call(
            functools.partial(split_kernel, dp), "split", "shv v" + "v" * (dp - 1), mac // 8,
            [q, full, got],
            [like(F32, *piece)] + [like(BF16, *piece)] * (dp - 1),
            [like(F32, *send.shape)], copies=levels,
        )
    got = [lax.ppermute(s, "dp", [(i, peer(i, k, dp)) for i in range(dp)]) for k, s in enumerate(sends, 1)]
    cross = lax.ppermute(cross, "seq", down)
    back, token = call(
        functools.partial(back_top_kernel, rows, width), "back_top", "hh h", 9 * mac, [low, sw], [rows_of(height)],
        [rows_of(height // 2 + 2), sw, rows_of(height // 2), wide(height // 2)], copies=3, after=[token],
    )
    level_piece = (rs + rt, chans)
    own, *sends, token = call(
        functools.partial(level_kernel, levels), "level", "sv" + "v" * (dp - 1) + " " + "v" * levels, mac // 8,
        [level, own, *got], [like(F32, *level_piece)] + [like(BF16, *level_piece)] * (levels - 1),
        after=[token],
    )
    got = [
        lax.ppermute(s, "seq", [(i, 2 * peer(i // 2, k, levels) + i % 2) for i in range(seq)])
        for k, s in reversed(list(enumerate(sends, 1)))
    ]
    back, token = call(
        functools.partial(back_bottom_kernel, rows, width), "back_bottom", "hhhh h", 9 * mac,
        [low, cross, sw, back], [rows_of(height)],
        [rows_of(height // 2 + 2), rows_of(REMOTE), sw, rows_of(height // 2), wide(height // 2)],
        copies=4, after=[token], alias={3: 0},
    )
    small, token = call(
        sum_kernel, "sum", "v" * levels + " v", mac // 8, [own, *got], [like(BF16, *level_piece)], after=[token]
    )
    got = [lax.ppermute(small, "dp", [(peer(i, k, dp), i) for i in range(dp)]) for k in range(1, dp)]
    spatial, temporal, token = call(
        functools.partial(place_kernel, scale), "place", "s" + "v" * dp + " vv", mac // 8, [q, small, *got],
        [like(F32, dp, rs, chans), like(F32, dp, rt, chans)],
    )
    return (back.reshape(video.shape), spatial.reshape(-1, chans), temporal.reshape(-1, chans))


def solution(mesh):
    placed = (P("dp", "seq", None, None, None), P("dp", "seq", None, None, None), P(), P())
    return jax.shard_map(
        shards,
        mesh=mesh,
        in_specs=placed,
        out_specs=(P("dp", "seq", None, None, None), P("seq", None), P("seq", None)),
        check_vma=False,
    )
```

```python
import functools

import jax
import jax.numpy as jnp
from jax import lax
from jax.experimental import pallas as pl
from jax.experimental.pallas import tpu as pltpu
from jax.sharding import PartitionSpec as P

BF16, F32 = jnp.bfloat16, jnp.float32
EDGE = 8
LIMIT, FULL = 24 * 2**20, 60 * 2**20
REMOTE = 7
SPARE = 45056


def dot(a, b):
    return jnp.dot(a, b, preferred_element_type=F32)


def dot_rt(a, b):
    return lax.dot_general(a, b, (((1,), (1,)), ((), ())), preferred_element_type=F32)


def dot_lt(a, b):
    return lax.dot_general(a, b, (((0,), (0,)), ((), ())), preferred_element_type=F32)


def like(dtype, *shape):
    return jax.ShapeDtypeStruct(shape, dtype)


SPACE = {
    "s": pl.BlockSpec(memory_space=pltpu.SMEM),
    "v": pl.BlockSpec(memory_space=pltpu.VMEM),
    "h": pl.BlockSpec(memory_space=pl.ANY),
}


def call(kernel, name, spaces, flops, args, outs, scratch=(), copies=0, after=(), alias=None, limit=LIMIT):
    nbytes = sum(a.size * a.dtype.itemsize for a in (*args, *outs) if a.shape[0] < SPARE)
    ins, results = spaces.split()
    n_in, n_out = len(args), len(outs)

    def body(*refs):
        rest = refs[n_in + len(after) :]
        kernel(*refs[:n_in], *rest[:n_out], *rest[n_out + 1 :])

    return pl.pallas_call(
        body,
        out_shape=[*outs, TOKEN],
        in_specs=[SPACE[c] for c in ins] + [SPACE["h"]] * len(after),
        out_specs=[SPACE[c] for c in results] + [SPACE["h"]],
        scratch_shapes=[*(pltpu.VMEM(s.shape, s.dtype) for s in scratch), *([pltpu.SemaphoreType.DMA((copies,))] if copies else [])],
        input_output_aliases={} if alias is None else alias,
        compiler_params=pltpu.CompilerParams(vmem_limit_bytes=limit),
        cost_estimate=pl.CostEstimate(flops=flops, bytes_accessed=nbytes, transcendentals=0),
        name=name,
    )(*args, *after)


class Copies:
    def __init__(self, sems):
        self.sems, self.used = sems, 0

    def start(self, *pairs):
        started = []
        for a, b in pairs:
            started.append(pltpu.make_async_copy(a, b, self.sems.at[self.used]))
            self.used += 1
            started[-1].start()
        return started


def wait_all(copies):
    for c in copies:
        c.wait()


def behind(value, token):
    return lax.optimization_barrier((value, token))


TOKEN = like(F32, 8, 128)


def tile(i, size, base=0):
    return pl.ds(pl.multiple_of(base + i * size, size), size)


def loop(steps, body):
    def step(i, carry):
        body(i)
        return carry

    lax.fori_loop(0, steps, step, 0)


def chunk(n):
    return n if n < 10 else max(d for d in range(1, 7) if n % d == 0)


def silu_parts(v):
    v = v.astype(F32)
    sig = 0.5 * jnp.tanh(0.5 * v) + 0.5
    act = v * sig
    return act.astype(BF16), sig + act * (1.0 - sig)


def clear_edges(pad):
    n, long, chans = pad.shape
    pad[:, :EDGE] = jnp.zeros((n, EDGE, chans), F32)
    pad[:, long - EDGE :] = jnp.zeros((n, EDGE, chans), F32)


def put_shifts(cat, where, mid, pad):
    n, long, chans = pad.shape
    width = long - 2 * EDGE
    pad[:, EDGE : EDGE + width] = mid.astype(F32).reshape(n, width, chans)
    cat[where, chans : 2 * chans] = mid
    cat[where, :chans] = pad[:, EDGE + 1 : EDGE + 1 + width].astype(BF16).reshape(n * width, chans)
    cat[where, 2 * chans :] = pad[:, EDGE - 1 : EDGE - 1 + width].astype(BF16).reshape(n * width, chans)


def conv_rows(rows3, tap, out, step, wide):
    width = wide.shape[2] - 2 * EDGE

    def body(i):
        start = i * step
        rows = [rows3[pl.ds(pl.multiple_of(start + a * width, width), step)] for a in range(3)]
        conv_tile(jnp.concatenate(rows, axis=1), tap, out, tile(i, step), wide)

    for side in range(2):
        clear_edges(wide.at[side])
    loop((rows3.shape[0] - 2 * width) // step, body)


def conv_tile(rows, tap, out, where, wide):
    _, n, long, chans = wide.shape
    width = long - 2 * EDGE
    wide[0, :, EDGE : EDGE + width] = tap(rows, 0).reshape(n, width, chans)
    wide[1, :, EDGE : EDGE + width] = tap(rows, 2).reshape(n, width, chans)
    mid = tap(rows, 1).reshape(n, width, chans)
    mid += wide[0, :, EDGE - 1 : EDGE - 1 + width] + wide[1, :, EDGE + 1 : EDGE + 1 + width]
    out[where] = mid.reshape(n * width, chans).astype(BF16)


def forward_tap(sw):
    return lambda rows, b: dot(rows, jnp.concatenate([sw[a, b] for a in range(3)], axis=0))


def back_tap(sw):
    return lambda rows, b: dot_rt(rows, jnp.concatenate([sw[2 - a, 2 - b] for a in range(3)], axis=1))


def tap_parts(video, cat, first, last, base, height, width):
    chans = video.shape[1]
    for a in range(3):
        low, high = max(first, 1 - a), min(last, height + 1 - a)
        rows = video[(low + a - 1 - base) * width : (high + a - 1 - base) * width]
        part = dot_lt(rows, cat[(low - first) * width : (high - first) * width])
        for b in range(3):
            yield 3 * a + b, part[:, b * chans : (b + 1) * chans]


def local_kernel(
    height, width, upper, core, video, cot, mate, sw, tw, act_top, slope_top, rest, cross, spatial, temporal, sw_v, low,
    rows3, both, tw_v, hidden_v, act, cat, wide, pad, grad_v, sems,
):
    rows, chans = video.shape
    top_rows = upper * width
    copies = Copies(sems)
    head = copies.start((video, rows3.at[width : rows + width]), (sw, sw_v))
    tail = copies.start((cot, both.at[:, :chans]), (mate, both.at[:, chans:]), (tw, tw_v))
    rows3[:width] = jnp.zeros((width, chans), BF16)
    rows3[rows + width :] = jnp.zeros((width, chans), BF16)
    clear_edges(pad)
    wait_all(head)
    conv_rows(rows3, forward_tap(sw_v), hidden_v, wide.shape[1] * width, wide)
    wait_all(tail)
    even = core[0] == 0
    tap0 = tw_v[0]
    tap1 = jnp.where(even, tw_v[1], jnp.zeros_like(tap0))
    taps = jnp.concatenate([tap0, tap1], axis=1)
    taps_cross = jnp.concatenate([tw_v[2], jnp.where(even, jnp.zeros_like(tap0), tw_v[1])], axis=1)
    step = pad.shape[0] * width

    def bottom(i):
        here = pl.ds(pl.multiple_of(top_rows + i * step, width), step)
        act_rows, slope = silu_parts(hidden_v[here])
        act[here] = act_rows
        pair = both[here]
        mid = (dot_rt(pair, taps) * slope).astype(BF16)
        cross[tile(i, step)] = dot_rt(pair, taps_cross)
        grad_v[tile(i, step)] = mid
        put_shifts(cat, tile(i, step), mid, pad)

    loop((rows - top_rows) // step, bottom)
    out = copies.start((grad_v, low.at[rows + top_rows : 2 * rows]))
    top_step = chunk(upper) * width

    def top(i):
        here = tile(i, top_step)
        act_rows, slope = silu_parts(hidden_v[here])
        act[here] = act_rows
        act_top[here] = act_rows
        slope_top[here] = slope
        rest[here] = dot_rt(both[here], taps)

    loop(top_rows // top_step, top)
    for tap, part in tap_parts(rows3, cat, upper, height, -1, height, width):
        spatial[tap] = part
    part = dot_lt(act[...], both[...])
    temporal[0] = part[:, :chans]
    temporal[1] = jnp.where(even, part[:, chans:], 0.0)
    temporal[2] = jnp.zeros((chans, chans), F32)
    wait_all(out)


def remote_kernel(
    height, width, upper, core, above, cot, mate, part, sw, spatial, temporal, spatial_out, temporal_out, grad,
    both, other, act, cat, wide, pad, grad_v, sems,
):
    chans = cot.shape[1]
    at = upper * width
    count = part.shape[0]
    copies = Copies(sems)
    tail = copies.start((mate.at[at:], both.at[:, :chans]), (cot.at[at:], both.at[:, chans:]))
    even = core[0] == 0
    clear_edges(pad)
    for side in range(2):
        clear_edges(wide.at[side])
    last = jnp.concatenate([above[2 * width :], jnp.zeros((width, chans), BF16)], axis=0)
    rows = jnp.concatenate([above[:count], above[width : width + count], last], axis=1)
    conv_tile(rows, forward_tap(sw), other, slice(0, count), wide)
    step = pad.shape[0] * width

    def remote(i):
        here = tile(i, step)
        act_rows, slope = silu_parts(other[here])
        act[here] = act_rows
        mid = (part[here] * slope).astype(BF16)
        grad_v[here] = mid
        put_shifts(cat, here, mid, pad)

    loop(count // step, remote)
    out = copies.start((grad_v, grad))
    for tap, part in tap_parts(above, cat, upper, height, upper - 1, height, width):
        spatial_out[tap] = spatial[tap] + part
    wait_all(tail)
    part = dot_lt(act[...], both[...])
    temporal_out[0] = temporal[0]
    temporal_out[1] = temporal[1] + jnp.where(even, 0.0, part[:, :chans])
    temporal_out[2] = temporal[2] + part[:, chans:]
    wait_all(out)


def own_kernel(
    height, width, upper, plain, core, video, act, slope, rest, near, far, tw, spatial, temporal, low_in, low, full, send,
    rows, cat, pad, grad_v, total, total_t, send_v, sems,
):
    count, chans = near.shape
    whole = height * width
    copies = Copies(sems)
    tail = copies.start((video.at[: count + width], rows))
    clear_edges(pad)
    even = core[0] == 0
    taps = jnp.concatenate([jnp.where(even, jnp.zeros_like(tw[1]), tw[1]), tw[2]], axis=1)
    step = pad.shape[0] * width

    def own(i):
        here = tile(i, step)
        grad = rest[here] + dot_rt(jnp.concatenate([near[here], far[here]], axis=1), taps)
        mid = (grad * slope[here]).astype(BF16)
        grad_v[here] = mid
        put_shifts(cat, here, mid, pad)

    loop(count // step, own)
    out = copies.start((grad_v, low.at[whole : whole + count]))
    part = dot_lt(act[...], jnp.concatenate([near[...], far[...]], axis=1))
    total_t[:chans] = temporal[0]
    total_t[chans : 2 * chans] = temporal[1] + jnp.where(even, 0.0, part[:, :chans])
    total_t[2 * chans :] = temporal[2] + part[:, chans:]
    n, first = total.shape[0], 0
    wait_all(tail)
    levels, each = send.shape[:2]
    rt = total_t.shape[0] // (2 * levels)
    rs = each - rt
    for tap, part in tap_parts(rows, cat, 0, upper, 0, height, width):
        total[tap * chans : (tap + 1) * chans] = spatial[tap] + part
        while not plain and first < levels and (first + 1) * 2 * rs <= (tap + 1) * chans:
            theirs, ours = 2 * first + 1 - core[0], 2 * first + core[0]
            send_v[first, :rs] = total[pl.ds(pl.multiple_of(theirs * rs, 8), rs)].astype(BF16)
            send_v[first, rs:] = total_t[pl.ds(pl.multiple_of(theirs * rt, 8), rt)].astype(BF16)
            at = first * each
            out += copies.start(
                (send_v.at[first], send.at[first]),
                (total.at[pl.ds(pl.multiple_of(ours * rs, 8), rs)], full.at[at : at + rs]),
                (total_t.at[pl.ds(pl.multiple_of(ours * rt, 8), rt)], full.at[at + rs : at + each]),
            )
            first += 1
    if plain:
        out += copies.start((total, full.at[:n]), (total_t, full.at[n : n + total_t.shape[0]]))
    wait_all(out)


def back_top_kernel(whole, width, low, sw, back, rows3, sw_v, out, wide, sems):
    chans = out.shape[1]
    held = rows3.shape[0] - width
    copies = Copies(sems)
    head = copies.start((low.at[whole : whole + held], rows3.at[width:]), (sw, sw_v))
    rows3[:width] = jnp.zeros((width, chans), BF16)
    wait_all(head)
    conv_rows(rows3, back_tap(sw_v), out, wide.shape[1] * width, wide)
    wait_all(copies.start((out, back.at[: out.shape[0]])))


def back_bottom_kernel(whole, width, low, got, sw, _, back, rows3, got_v, sw_v, out, wide, sems):
    chans = out.shape[1]
    held = rows3.shape[0] - width
    count = got.shape[0]
    copies = Copies(sems)
    head = copies.start((low.at[2 * whole - held : 2 * whole], rows3.at[:held]), (sw, sw_v))
    head += copies.start((got, got_v))
    rows3[held:] = jnp.zeros((width, chans), BF16)
    wait_all(head)

    def add(i):
        here = pl.ds(pl.multiple_of(held - count + i * width, width), width)
        rows3[here] = (rows3[here].astype(F32) + got_v[tile(i, width)].astype(F32)).astype(BF16)

    loop(count // width, add)
    conv_rows(rows3, back_tap(sw_v), out, wide.shape[1] * width, wide)
    wait_all(copies.start((out, back.at[back.shape[0] - out.shape[0] :])))


def peer(index, k, size):
    return index ^ k if size & (size - 1) == 0 else (index + k) % size


def split_kernel(size, where, kept, swapped, own, *refs):
    sends, (keep_v, sems) = refs[: size - 1], refs[size - 1 :]
    q = where[0]
    levels, each, chans = swapped.shape
    rs = own.shape[1] * 3 // 4
    rt = own.shape[1] - rs
    copies = Copies(sems)
    ins = copies.start(*((kept.at[level * each : (level + 1) * each], keep_v.at[level]) for level in range(levels)))
    for level in range(levels):
        ins[level].wait()
        keep_v[level] += swapped[level].astype(F32)

        def total(i):
            low = keep_v[level, pl.ds(pl.multiple_of(i * rs, 8), rs)]
            return jnp.concatenate([low, keep_v[level, pl.ds(pl.multiple_of(size * rs + i * rt, 8), rt)]], axis=0)

        for k, send in enumerate(sends):
            send[level] = total(peer(q, k + 1, size)).astype(BF16)
        own[level] = total(q)


def level_kernel(size, where, own, *refs):
    got = refs[:-size]
    mine, *sends = refs[-size:]
    level = where[0]

    def total(i):
        return sum((g[i].astype(F32) for g in got), own[i])

    mine[...] = total(level)
    for k, out in enumerate(sends, 1):
        out[...] = total(peer(level, k, size)).astype(BF16)


def sum_kernel(own, *refs):
    *got, out = refs
    out[...] = sum((g[...].astype(F32) for g in got), own[...]).astype(BF16)


def place_kernel(scale, where, small, *refs):
    *got, spatial, temporal = refs
    size, rs, rt = len(got) + 1, spatial.shape[1], temporal.shape[1]
    for k, part in enumerate((small, *got)):
        at = peer(where[0], k, size)
        rows = part[...].astype(F32) * scale
        spatial[at] = rows[:rs]
        temporal[at] = rows[rs:]


def shards(video, cotangent, spatial_weight, temporal_weight):
    height, width, chans = (video.shape[2], video.shape[3], video.shape[4])
    rows = height * width
    dp, seq = lax.axis_size("dp"), lax.axis_size("seq")
    levels = seq // 2
    scale = float((dp * video.shape[0] * seq * rows) ** -0.5)
    dp_at, seq_at = lax.axis_index("dp").astype(jnp.int32), lax.axis_index("seq").astype(jnp.int32)
    core, level, q = (v.reshape(1) for v in (seq_at % 2, seq_at // 2, dp_at))
    x = video.reshape(rows, chans)
    cot = cotangent.reshape(rows, chans)
    sw, tw = spatial_weight, temporal_weight
    upper = height - REMOTE
    down = [(i + 2, i) for i in range(seq - 2)]
    up = [(i, i + 2) for i in range(seq - 2)]
    swap = [(i, i ^ 1) for i in range(seq)]

    mac = rows * chans * chans
    long = width + 2 * EDGE
    taps9, taps3 = (like(F32, n, chans, chans) for n in (9, 3))

    def rows_of(n, columns=chans, dtype=BF16):
        return like(dtype, n * width, columns)

    def wide(n):
        return like(F32, 2, n, long, chans)

    mate = lax.ppermute(cot, "seq", swap)
    far = lax.ppermute(cot[: upper * width], "seq", down)
    above, mate = lax.optimization_barrier((x[(upper - 1) * width :], mate))
    above = lax.ppermute(above, "seq", up)

    def pad(n):
        return like(F32, n, long, chans)

    act, slope, rest, part, spatial, temporal, sw_v, low, token = call(
        functools.partial(local_kernel, height, width, upper), "local", "shhhhh vvvvvvvh", 34 * mac, [core, x, cot, mate, sw, tw],
        [
            rows_of(upper), rows_of(upper, dtype=F32), rows_of(upper, dtype=F32), rows_of(REMOTE, dtype=F32), taps9, taps3, sw,
            like(BF16, 2 * SPARE, chans),
        ],
        [
            rows_of(height + 2), rows_of(height, 2 * chans), tw, rows_of(height), rows_of(height),
            rows_of(REMOTE, 3 * chans), wide(height // 2), pad(chunk(REMOTE)), rows_of(REMOTE),
        ],
        copies=6,
    )
    far, token = behind(far, token)
    near = lax.ppermute(far, "seq", swap)
    spatial, temporal, cross, token = call(
        functools.partial(remote_kernel, height, width, upper), "remote", "svhhvvvv vvh", 16 * mac,
        [core, above, cot, mate, part, sw_v, spatial, temporal], [taps9, taps3, rows_of(REMOTE)],
        [
            rows_of(REMOTE, 2 * chans), rows_of(REMOTE), rows_of(REMOTE),
            rows_of(REMOTE, 3 * chans), wide(REMOTE), pad(chunk(REMOTE)), rows_of(REMOTE),
        ],
        copies=3, after=[token],
    )
    rs, rt = 9 * chans // (seq * dp), 3 * chans // (seq * dp)
    plain = bool(rs % 8 or rt % 8 or dp * rs % 16 or dp * rt % 16)
    send = like(BF16, levels, dp * (rs + rt), chans)
    low, full, send, token = call(
        functools.partial(own_kernel, height, width, upper, plain), "own", "shvvvvvvvvh hhh", 16 * mac,
        [core, x, act, slope, rest, near, far, tw, spatial, temporal, low], [low, like(F32, SPARE, chans), send],
        [
            rows_of(upper + 1), rows_of(upper, 3 * chans), pad(chunk(upper)),
            rows_of(upper), like(F32, 9 * chans, chans), like(F32, 3 * chans, chans), send,
        ],
        copies=4 + 3 * levels, after=[token], alias={10: 0},
    )
    piece = (levels, rs + rt, chans)
    if plain:
        parts = (full[: 9 * chans], full[9 * chans : 12 * chans])
        both = jnp.concatenate([g.reshape(levels, 2, dp, -1, chans) for g in parts], axis=3)
        pick = functools.partial(lax.dynamic_index_in_dim, keepdims=False)
        got = lax.ppermute(pick(both, 1 - core[0], 1).astype(BF16), "seq", swap)
        mine = pick(both, core[0], 1) + got.astype(F32)
        own = pick(mine, q[0], 1)
        sends = [pick(mine, peer(q[0], k, dp), 1).astype(BF16) for k in range(1, dp)]
    else:
        got = lax.ppermute(send, "seq", swap)
        own, *sends, token = call(
            functools.partial(split_kernel, dp), "split", "shv v" + "v" * (dp - 1), mac // 8,
            [q, full, got],
            [like(F32, *piece)] + [like(BF16, *piece)] * (dp - 1),
            [like(F32, *send.shape)], copies=levels,
        )
    got = [lax.ppermute(s, "dp", [(i, peer(i, k, dp)) for i in range(dp)]) for k, s in enumerate(sends, 1)]
    cross = lax.ppermute(cross, "seq", down)
    back, token = call(
        functools.partial(back_top_kernel, rows, width), "back_top", "hh h", 9 * mac, [low, sw], [rows_of(height)],
        [rows_of(height // 2 + 2), sw, rows_of(height // 2), wide(height // 2)], copies=3, after=[token],
    )
    level_piece = (rs + rt, chans)
    own, *sends, token = call(
        functools.partial(level_kernel, levels), "level", "sv" + "v" * (dp - 1) + " " + "v" * levels, mac // 8,
        [level, own, *got], [like(F32, *level_piece)] + [like(BF16, *level_piece)] * (levels - 1),
        after=[token],
    )
    got = [
        lax.ppermute(s, "seq", [(i, 2 * peer(i // 2, k, levels) + i % 2) for i in range(seq)])
        for k, s in sorted(enumerate(sends, 1), key=lambda pair: (pair[0] < levels // 2, pair[0]))
    ]
    back, token = call(
        functools.partial(back_bottom_kernel, rows, width), "back_bottom", "hhhh h", 9 * mac,
        [low, cross, sw, back], [rows_of(height)],
        [rows_of(height // 2 + 2), rows_of(REMOTE), sw, rows_of(height // 2), wide(height // 2)],
        copies=4, after=[token], alias={3: 0},
    )
    small, token = call(
        sum_kernel, "sum", "v" * levels + " v", mac // 8, [own, *got], [like(BF16, *level_piece)], after=[token]
    )
    got = [lax.ppermute(small, "dp", [(peer(i, k, dp), i) for i in range(dp)]) for k in range(1, dp)]
    spatial, temporal, token = call(
        functools.partial(place_kernel, scale), "place", "s" + "v" * dp + " vv", mac // 8, [q, small, *got],
        [like(F32, dp, rs, chans), like(F32, dp, rt, chans)],
    )
    return (back.reshape(video.shape), spatial.reshape(-1, chans), temporal.reshape(-1, chans))


def solution(mesh):
    placed = (P("dp", "seq", None, None, None), P("dp", "seq", None, None, None), P(), P())
    return jax.shard_map(
        shards,
        mesh=mesh,
        in_specs=placed,
        out_specs=(P("dp", "seq", None, None, None), P("seq", None), P("seq", None)),
        check_vma=False,
    )
```
